32 devices in a mesh: dp: 2 (over core), seq: 16 (over z, y, x).
Axes of the slice: x: 2, y: 2, z: 4, core: 2. Of those that a mesh axis runs over, the one named last changes fastest.
Arguments:
- queries: bfloat16 [2, 2048, 1024], P('dp', 'seq'), may hold values from -5 to 5
- keys: bfloat16 [2, 2048, 1024], P('dp', 'seq'), may hold values from -5 to 5
- values: bfloat16 [2, 2048, 1024], P('dp', 'seq'), may hold values from -6 to 6
- out_grad: bfloat16 [2, 2048, 1024], P('dp', 'seq'), may hold values from -6 to 6
- out_weight: bfloat16 [1024, 1024], P('dp'), may hold values from -0.1875 to 0.1875
- band_width: int32 [4], replicated, may hold values from 1 to 4, as said below
- col_reach: int32 [4], replicated, may hold values from 2 to 4, as said below
Outputs:
- query_grad: bfloat16 [2, 2048, 1024], P('dp', 'seq')
- key_grad: bfloat16 [2, 2048, 1024], P('dp', 'seq')
- value_grad: bfloat16 [2, 2048, 1024], P('dp', 'seq')
- weight_grad: bfloat16 [1024, 1024], P('dp')
The draws below stay inside these ranges and needn't reach their ends.
Inputs may be any that keep to these rules, and one draw needn't show every extreme that they name: `band_width`: some band head has width exactly 4. `col_reach`: some strided head reaches all 4 rows.
All inputs are finite; a program needn't handle non-finite values.
Results may differ from the reference program's by a relative error of at most 0.019.
Values may be sent and summed in bfloat16 or wider, within the bound.
No kernel may reach another device: no remote copies, remote signals or barrier semaphores. Data moves between devices by JAX's collectives and lax.ppermute only.
A program may use at most 64 MiB of HBM per device.

```python
import jax
import jax.numpy as jnp
from jax import lax

HD = 128
HB = 4
HS = 4
IMW = 512
BLK = 128
WMAX = 4
D = 1024
BATCH = 2
L = 2048
NR = 4


def drawn_fields(key):
    shape = (BATCH, L, D)
    query_field = jnp.clip(jax.random.normal(jax.random.fold_in(key, 11), shape, jnp.float32), -4.0, 4.0)
    key_field = jnp.clip(jax.random.normal(jax.random.fold_in(key, 12), shape, jnp.float32), -4.0, 4.0)
    return (query_field, key_field)


def draw_queries(key, part):
    return drawn_fields(key)[0].astype(jnp.bfloat16)


def draw_keys(key, part):
    return drawn_fields(key)[1].astype(jnp.bfloat16)


def draw_band_width(key, part):
    widths = jax.random.randint(jax.random.fold_in(key, 21), (HB,), 1, WMAX)
    chosen = jax.random.randint(jax.random.fold_in(key, 22), (), 0, HB)
    return jnp.where(jnp.arange(HB) == chosen, WMAX, widths).astype(jnp.int32)


def draw_col_reach(key, part):
    lowest = max(NR // 4, 2)
    reaches = jax.random.randint(jax.random.fold_in(key, 31), (HS,), lowest, NR)
    chosen = jax.random.randint(jax.random.fold_in(key, 32), (), 0, HS)
    return jnp.where(jnp.arange(HS) == chosen, NR, reaches).astype(jnp.int32)


def with_spikes(entries, key, source, target, shards_of, factor):
    owner, partner = [(jnp.arange(entries.shape[axis_at]) // (entries.shape[axis_at] // shards_of)).reshape([-1 if axis == axis_at else 1 for axis in range(entries.ndim)]) for axis_at in (source, target)]
    chosen = jax.random.permutation(key, shards_of)[partner]
    strong = (owner == chosen) | (owner == (partner + shards_of // 2) % shards_of)
    return jnp.where(strong, factor * entries, entries)


def steps_of(stream_key, extent, cuts, least, high):
    gain = 1.0
    for dim, blocks in cuts:
        heights = jax.random.uniform(jax.random.fold_in(jax.random.fold_in(stream_key, 6), dim), (blocks,), jnp.float32, least / len(cuts), high / len(cuts))
        gain = gain * jnp.repeat(jnp.exp(heights), extent[dim] // blocks).reshape((-1,) + (1,) * (len(extent) - 1 - dim))
    return gain


def centred(stream_key, dims, scale, most, split=(), held_as=jnp.bfloat16):
    values = scale * jax.random.normal(stream_key, dims, jnp.float32)
    if split:
        values = values * steps_of(stream_key, dims, split, -0.22, 0.18)
    return jnp.clip(values, -most, most).astype(held_as)


def bell_draw_with(key, shape, scale, most, shards, heavy, kind=jnp.bfloat16):
    drawn = scale * jax.random.normal(key, shape, jnp.float32)
    if shards:
        drawn = drawn * steps_of(key, shape, shards, -0.22, 0.18)
    return jnp.clip(with_spikes(drawn, jax.random.fold_in(key, 3), *heavy), -most, most).astype(kind)


def setup_inputs(seed: int = 0) -> dict:
    key_of = jax.random.split(jax.random.key(seed), 8)
    return {
        "queries": draw_queries(jax.random.fold_in(key_of[7], 71), 0),
        "keys": draw_keys(jax.random.fold_in(key_of[7], 71), 0),
        "values": centred(key_of[2], (BATCH, L, D), 1.0, 6.0, ((0, 2), (1, 16))),
        "out_grad": bell_draw_with(key_of[3], (BATCH, L, D), 1.0, 6.0, ((0, 2), (1, 16)), (1, 2, 16, 2.0)),
        "out_weight": centred(key_of[4], (D, D), D ** -0.5, 0.1875, ((0, 2),)),
        "band_width": draw_band_width(jax.random.fold_in(key_of[7], 71), 0),
        "col_reach": draw_col_reach(jax.random.fold_in(key_of[7], 71), 0),
    }


def lowered(field):
    return lax.optimization_barrier(field.astype(jnp.bfloat16))


def attend(query_g, key_g, value_g, grad_g, allowed):
    scale = query_g.shape[-1] ** -0.5
    query_w = query_g.astype(jnp.float32)
    key_w = key_g.astype(jnp.float32)
    value_w = value_g.astype(jnp.float32)
    grad_w = grad_g.astype(jnp.float32)
    scores = jnp.einsum('gqd,gkd->gqk', query_w, key_w) * scale
    scores = jnp.where(allowed, scores, -1e30)
    peak = jnp.max(scores, axis=-1, keepdims=True)
    raised = jnp.where(allowed, jnp.exp(scores - peak), 0.0)
    probs = raised / jnp.sum(raised, axis=-1, keepdims=True)
    probs_low = lowered(probs)
    probs_wide = probs_low.astype(jnp.float32)
    output = lowered(jnp.einsum('gqk,gkd->gqd', probs_wide, value_w))
    delta = jnp.sum(grad_w * output.astype(jnp.float32), axis=-1, keepdims=True)
    dprobs = jnp.einsum('gqd,gkd->gqk', grad_w, value_w)
    dscores = lowered(probs * (dprobs - delta)).astype(jnp.float32)
    d_query = jnp.einsum('gqk,gkd->gqd', dscores, key_w) * scale
    d_key = jnp.einsum('gqk,gqd->gkd', dscores, query_w) * scale
    d_value = jnp.einsum('gqk,gqd->gkd', probs_wide, grad_w)
    return output, d_query, d_key, d_value


def band_mask(q_pos, k_pos, width):
    lower = (q_pos // BLK)[None, :, None] - width[:, None, None]
    causal = k_pos[None, None, :] <= q_pos[None, :, None]
    inside = k_pos[None, None, :] >= 0
    return causal & inside & ((k_pos // BLK)[None, None, :] >= lower)


def column_mask(count, reach):
    row_q = jnp.arange(count, dtype=jnp.int32)[None, :, None]
    row_k = jnp.arange(count, dtype=jnp.int32)[None, None, :]
    return (row_k <= row_q) & (row_q - row_k < reach[:, None, None])


def band_part(query_b, key_b, value_b, grad_b, width):
    nblk = L // BLK
    span = (WMAX + 1) * BLK
    band_dim = HB * HD
    padding = jnp.zeros((WMAX * BLK, band_dim), key_b.dtype)
    key_pad = jnp.concatenate([padding, key_b], 0)
    value_pad = jnp.concatenate([padding, value_b], 0)

    def heads_first(field, count):
        return field.reshape(count, HB, HD).transpose(1, 0, 2)

    def one_block(index):
        start = index * BLK
        query_blk = heads_first(lax.dynamic_slice_in_dim(query_b, start, BLK, 0), BLK)
        grad_blk = heads_first(lax.dynamic_slice_in_dim(grad_b, start, BLK, 0), BLK)
        key_win = heads_first(lax.dynamic_slice_in_dim(key_pad, start, span, 0), span)
        value_win = heads_first(lax.dynamic_slice_in_dim(value_pad, start, span, 0), span)
        q_pos = start + jnp.arange(BLK, dtype=jnp.int32)
        k_pos = (index - WMAX) * BLK + jnp.arange(span, dtype=jnp.int32)
        allowed = band_mask(q_pos, k_pos, width)
        return attend(query_blk, key_win, value_win, grad_blk, allowed)

    output, d_query, d_key, d_value = lax.map(one_block, jnp.arange(nblk, dtype=jnp.int32))

    def rows_back(field):
        return field.transpose(0, 2, 1, 3).reshape(L, band_dim)

    def spread(field):
        pieces = field.reshape(nblk, HB, WMAX + 1, BLK, HD)
        padded = jnp.zeros((nblk + WMAX, HB, BLK, HD), jnp.float32)
        for offset in range(WMAX + 1):
            padded = padded.at[offset:offset + nblk].add(pieces[:, :, offset])
        return rows_back(padded[WMAX:])

    return rows_back(output), rows_back(d_query), spread(d_key), spread(d_value)


def column_part(query_s, key_s, value_s, grad_s, reach):
    count = L // IMW

    def to_groups(field):
        return field.reshape(count, IMW, HS, HD).transpose(1, 2, 0, 3).reshape(IMW * HS, count, HD)

    def from_groups(field):
        return field.reshape(IMW, HS, count, HD).transpose(2, 0, 1, 3).reshape(L, HS * HD)

    allowed = jnp.tile(column_mask(count, reach), (IMW, 1, 1))
    results = attend(to_groups(query_s), to_groups(key_s), to_groups(value_s), to_groups(grad_s), allowed)
    return tuple(from_groups(field) for field in results)


def reference(queries, keys, values, out_grad, out_weight, band_width, col_reach):
    band_dim = HB * HD
    query_list, key_list, value_list = [], [], []
    weight_total = jnp.zeros((D, D), jnp.float32)
    for member in range(BATCH):
        query_all = queries[member]
        key_all = keys[member]
        value_all = values[member]
        att_grad = lowered(jnp.dot(out_grad[member], out_weight.T, preferred_element_type=jnp.float32))
        band_out, band_dq, band_dk, band_dv = band_part(query_all[:, :band_dim], key_all[:, :band_dim], value_all[:, :band_dim], att_grad[:, :band_dim], band_width)
        col_out, col_dq, col_dk, col_dv = column_part(query_all[:, band_dim:], key_all[:, band_dim:], value_all[:, band_dim:], att_grad[:, band_dim:], col_reach)
        attn_out = jnp.concatenate([band_out, col_out], 1)
        weight_total = weight_total + jnp.dot(attn_out.T, out_grad[member], preferred_element_type=jnp.float32)
        query_list.append(jnp.concatenate([band_dq, col_dq], 1).astype(jnp.bfloat16))
        key_list.append(jnp.concatenate([band_dk, col_dk], 1).astype(jnp.bfloat16))
        value_list.append(jnp.concatenate([band_dv, col_dv], 1).astype(jnp.bfloat16))
    return (jnp.stack(query_list), jnp.stack(key_list), jnp.stack(value_list), weight_total.astype(jnp.bfloat16))
```

```python
import functools

import jax
import jax.numpy as jnp
from jax import lax
from jax.experimental import pallas as pl
from jax.experimental.pallas import tpu as pltpu
from jax.sharding import PartitionSpec as P

HD = 128
HB = 4
HS = 4
IMW = 512
BLK = 128
WMAX = 4

BF = jnp.bfloat16
F32 = jnp.float32
MIB = 1 << 20


def nn(a, b):
    return lax.dot_general(a, b, (((1,), (0,)), ((), ())), preferred_element_type=F32)


def nt(a, b):
    return lax.dot_general(a, b, (((1,), (1,)), ((), ())), preferred_element_type=F32)


def tn(a, b):
    return lax.dot_general(a, b, (((0,), (0,)), ((), ())), preferred_element_type=F32)


def rows_at(start, size):
    return pl.ds(pl.multiple_of(start, size), size)


def shaped(shape, dtype=BF):
    return jax.ShapeDtypeStruct(shape, dtype)


def call(kernel, outs, args, smem=0, scratch=(), mib=16, name=None):
    vmem = pl.BlockSpec(memory_space=pltpu.VMEM)
    scalars = pl.BlockSpec(memory_space=pltpu.SMEM)
    return pl.pallas_call(
        kernel,
        out_shape=outs,
        in_specs=[scalars] * smem + [vmem] * (len(args) - smem),
        out_specs=[vmem] * len(outs),
        scratch_shapes=list(scratch),
        compiler_params=pltpu.CompilerParams(vmem_limit_bytes=mib * MIB),
        name=name,
    )(*args)


def roles(band, strided):
    role = lax.axis_index("dp")
    pl.when(role == 0)(band)
    pl.when(role == 1)(strided)


def spot(g):
    place = lax.axis_index("seq")
    return lax.div(place, g), lax.rem(place, g)


def pack_swap_kernel(q_ref, k_ref, v_ref, out_ref):
    half = out_ref.shape[2]

    def take(start):
        for t, ref in enumerate((q_ref, k_ref, v_ref)):
            out_ref[t] = ref[:, start : start + half]

    roles(lambda: take(half), lambda: take(0))


def pack_fields_kernel(g, q_ref, k_ref, v_ref, other_ref, *out_refs):
    line, spot_ = spot(g)
    rows, half = other_ref.shape[1:]
    chunk = rows // g
    own = (q_ref, k_ref, v_ref)

    def band():
        for d in range(1, g):
            lanes = rows_at((spot_ ^ d) * HD, HD)
            for t in range(3):
                out_refs[d - 1][t * rows : (t + 1) * rows] = own[t][:, lanes]
                out_refs[d - 1][(3 + t) * rows : (4 + t) * rows] = other_ref[t, :, lanes]

    def strided():
        for d in range(1, g):
            there = rows_at((line ^ d) * chunk, chunk)
            for t in range(3):
                for h in range(HS):
                    at = t * rows + h * chunk
                    out_refs[d - 1][at : at + chunk] = own[t][there, half + h * HD : half + (h + 1) * HD]
                    at += 3 * rows
                    out_refs[d - 1][at : at + chunk] = other_ref[t, there, h * HD : (h + 1) * HD]

    roles(band, strided)


def att_grad_kernel(own_ref, other_ref, weight_ref, out_ref):
    out_ref[0] = nt(own_ref[...], weight_ref[...]).astype(BF)
    out_ref[1] = nt(other_ref[...], weight_ref[...]).astype(BF)


def strided_mask(rows, chunk, reach):
    row = lax.broadcasted_iota(jnp.int32, (rows, rows), 0)
    col = lax.broadcasted_iota(jnp.int32, (rows, rows), 1)
    apart = lax.div(row, chunk) - lax.div(col, chunk)
    same = lax.rem(row, chunk) == lax.rem(col, chunk)
    return same & (apart >= 0) & (apart < reach)


def softmax(scores, allowed):
    scores = jnp.where(allowed, scores, -1e30)
    raised = jnp.exp(scores - jnp.max(scores, axis=-1, keepdims=True))
    raised = jnp.where(allowed, raised, 0.0)
    return raised * (1.0 / jnp.sum(raised, axis=-1, keepdims=True))


def forward_kernel(g, reach_ref, q_ref, k_ref, v_ref, other_ref, att_ref, r1_ref, r2_ref, r3_ref,
                   fq_ref, fkv_ref, o1_ref, o2_ref, o3_ref, keep_ref):
    line, spot_ = spot(g)
    rows, half = other_ref.shape[1:]
    span = g * rows
    chunk = rows // g
    own = (q_ref, k_ref, v_ref)
    came = (r1_ref, r2_ref, r3_ref)
    back = (o1_ref, o2_ref, o3_ref)

    def put(i, t, start, size, value):
        if t == 0:
            fq_ref[rows_at(i * span + start, size)] = value
        else:
            fkv_ref[rows_at((i * 2 + t - 1) * span + start, size)] = value

    def band():
        lanes = rows_at(spot_ * HD, HD)
        for t in range(3):
            put(0, t, spot_ * rows, rows, own[t][:, lanes])
            put(1, t, spot_ * rows, rows, other_ref[t, :, lanes])
            for d in range(1, g):
                for i in range(2):
                    at = (i * 3 + t) * rows
                    put(i, t, (spot_ ^ d) * rows, rows, came[d - 1][at : at + rows])
        for d in range(1, g):
            lanes = rows_at((spot_ ^ d) * HD, HD)
            for i in range(2):
                back[d - 1][(2 + i) * rows : (3 + i) * rows] = att_ref[i, :, lanes]

    def strided():
        here = rows_at(line * chunk, chunk)
        for t in range(3):
            for h in range(HS):
                put(0, t, h * rows + line * chunk, chunk, own[t][here, half + h * HD : half + (h + 1) * HD])
                put(1, t, h * rows + line * chunk, chunk, other_ref[t, here, h * HD : (h + 1) * HD])
                for d in range(1, g):
                    for i in range(2):
                        at = (i * 3 + t) * rows + h * chunk
                        put(i, t, h * rows + (line ^ d) * chunk, chunk, came[d - 1][at : at + chunk])
        for i in range(2):
            for h in range(HS):
                allowed = strided_mask(rows, chunk, reach_ref[h])
                at = i * span + h * rows
                query = fq_ref[at : at + rows]
                key = fkv_ref[i * span + at : i * span + at + rows]
                value = fkv_ref[(i + 1) * span + at : (i + 1) * span + at + rows]
                probs = softmax(nt(query, key) * (HD ** (-0.5)), allowed)
                keep_ref[i, h] = nn(probs.astype(BF), value).astype(BF)
        for d in range(1, g):
            there = rows_at((line ^ d) * chunk, chunk)
            for i in range(2):
                for h in range(HS):
                    at = (i * HS + h) * chunk
                    back[d - 1][at : at + chunk] = keep_ref[i, h, there]
                    at += 2 * rows
                    back[d - 1][at : at + chunk] = att_ref[i, there, h * HD : (h + 1) * HD]

    roles(band, strided)


def heads_kernel(g, keep_ref, o1_ref, o2_ref, o3_ref, p1_ref, p2_ref, p3_ref, mine_ref):
    line, spot_ = spot(g)
    rows = keep_ref.shape[2]
    chunk = rows // g
    came = (o1_ref, o2_ref, o3_ref)
    outs = (mine_ref, p1_ref, p2_ref, p3_ref)

    def strided():
        for to in range(g):
            head = spot_ ^ to
            for i in range(2):
                outs[to][rows_at(i * rows + line * chunk, chunk)] = keep_ref[i, head, rows_at(line * chunk, chunk)]
                for d in range(1, g):
                    source = rows_at((i * HS + head) * chunk, chunk)
                    outs[to][rows_at(i * rows + (line ^ d) * chunk, chunk)] = came[d - 1][source]

    roles(lambda: None, strided)


def gradients(query, key, value, grad, probs, output):
    probs_low = probs.astype(BF)
    delta = jnp.sum(grad.astype(F32) * output.astype(F32), axis=-1, keepdims=True)
    dscores = (probs * (nt(grad, value) - delta)).astype(BF)
    scale = HD ** (-0.5)
    return nn(dscores, key) * scale, tn(dscores, query) * scale, tn(probs_low, grad)


def attention_kernel(g, width_ref, reach_ref, fq_ref, fkv_ref, halo_ref, att_ref, o1_ref, o2_ref, o3_ref,
                     out_ref, grads_ref, tail_ref, grad_s, key_s, value_s, dkey_s, dvalue_s):
    line, spot_ = spot(g)
    rows = att_ref.shape[1]
    span = g * rows
    chunk = rows // g
    came = (o1_ref, o2_ref, o3_ref)
    scale = HD ** (-0.5)

    def band():
        width = width_ref[spot_]
        row = lax.broadcasted_iota(jnp.int32, (rows, span + rows), 0)
        col = lax.broadcasted_iota(jnp.int32, (rows, span + rows), 1)
        block = lax.div(col, BLK)
        near = (block >= WMAX - width) & (col - span <= row)
        for i in range(2):
            grad_s[rows_at(spot_ * rows, rows)] = att_ref[i, :, rows_at(spot_ * HD, HD)]
            for d in range(1, g):
                grad_s[rows_at((spot_ ^ d) * rows, rows)] = came[d - 1][(2 + i) * rows : (3 + i) * rows]
            key_s[:span] = halo_ref[i * 2 * span : (i * 2 + 1) * span]
            key_s[span:] = fkv_ref[i * 2 * span : (i * 2 + 1) * span]
            value_s[:span] = halo_ref[(i * 2 + 1) * span : (i * 2 + 2) * span]
            value_s[span:] = fkv_ref[(i * 2 + 1) * span : (i * 2 + 2) * span]
            dkey_s[...] = jnp.zeros_like(dkey_s)
            dvalue_s[...] = jnp.zeros_like(dvalue_s)
            for b in range(g):
                window = slice(b * rows, b * rows + span + rows)
                mine = slice(b * rows, (b + 1) * rows)
                at = i * span + b * rows
                query, grad = fq_ref[at : at + rows], grad_s[mine]
                key, value = key_s[window], value_s[window]
                allowed = near & ((block + b >= g) | (line > 0))
                probs = softmax(nt(query, key) * scale, allowed)
                output = nn(probs.astype(BF), value).astype(BF)
                out_ref[at : at + rows] = output
                dquery, dkey, dvalue = gradients(query, key, value, grad, probs, output)
                grads_ref[i, 0, mine] = dquery
                dkey_s[window] += dkey
                dvalue_s[window] += dvalue
            grads_ref[i, 1] = dkey_s[span:]
            grads_ref[i, 2] = dvalue_s[span:]
            tail_ref[i * 2 * span : (i * 2 + 1) * span] = dkey_s[:span].astype(BF)
            tail_ref[(i * 2 + 1) * span : (i * 2 + 2) * span] = dvalue_s[:span].astype(BF)

    def strided():
        for i in range(2):
            for h in range(HS):
                own = att_ref[i, rows_at(line * chunk, chunk), h * HD : (h + 1) * HD]
                grad_s[rows_at(h * rows + line * chunk, chunk)] = own
                for d in range(1, g):
                    at = 2 * rows + (i * HS + h) * chunk
                    grad_s[rows_at(h * rows + (line ^ d) * chunk, chunk)] = came[d - 1][at : at + chunk]
            for h in range(HS):
                allowed = strided_mask(rows, chunk, reach_ref[h])
                mine = slice(h * rows, (h + 1) * rows)
                at = i * span + h * rows
                query, grad = fq_ref[at : at + rows], grad_s[mine]
                key = fkv_ref[i * span + at : i * span + at + rows]
                value = fkv_ref[(i + 1) * span + at : (i + 1) * span + at + rows]
                probs = softmax(nt(query, key) * scale, allowed)
                output = nn(probs.astype(BF), value).astype(BF)
                dquery, dkey, dvalue = gradients(query, key, value, grad, probs, output)
                grads_ref[i, 0, mine] = dquery
                grads_ref[i, 1, mine] = dkey
                grads_ref[i, 2, mine] = dvalue

    roles(band, strided)


def pack_grads_kernel(g, grads_ref, tail_ref, keep_ref, r1_ref, r2_ref, r3_ref):
    line, spot_ = spot(g)
    span = grads_ref.shape[2]
    rows = span // g
    chunk = rows // g
    outs = (keep_ref, r1_ref, r2_ref, r3_ref)

    def band():
        for d in range(g):
            block = (spot_ ^ d) * rows
            for i in range(2):
                for t in range(3):
                    total = grads_ref[i, t, rows_at(block, rows)]
                    if t:
                        total += tail_ref[rows_at((i * 2 + t - 1) * span + block, rows)].astype(F32)
                    outs[d][(i * 3 + t) * rows : (i * 3 + t + 1) * rows] = total.astype(BF)

    def strided():
        for d in range(g):
            for i in range(2):
                for t in range(3):
                    for h in range(HS):
                        at = (i * 3 + t) * rows + h * chunk
                        there = rows_at(h * rows + (line ^ d) * chunk, chunk)
                        outs[d][at : at + chunk] = grads_ref[i, t, there].astype(BF)

    roles(band, strided)


def sort_grads_kernel(g, keep_ref, r1_ref, r2_ref, r3_ref, own_ref, other_ref):
    line, spot_ = spot(g)
    rows = own_ref.shape[1]
    chunk = rows // g
    came = (keep_ref, r1_ref, r2_ref, r3_ref)

    def band():
        for d in range(g):
            lanes = rows_at((spot_ ^ d) * HD, HD)
            for t in range(3):
                own_ref[t, :, lanes] = came[d][t * rows : (t + 1) * rows]
                other_ref[t, :, lanes] = came[d][(3 + t) * rows : (4 + t) * rows]

    def strided():
        for d in range(g):
            there = rows_at((line ^ d) * chunk, chunk)
            for t in range(3):
                for h in range(HS):
                    at = t * rows + h * chunk
                    own_ref[t, there, h * HD : (h + 1) * HD] = came[d][at : at + chunk]
                    at += 3 * rows
                    other_ref[t, there, h * HD : (h + 1) * HD] = came[d][at : at + chunk]

    roles(band, strided)


def join_grads_kernel(own_ref, other_ref, dq_ref, dk_ref, dv_ref):
    half = own_ref.shape[2]

    def join(left, right):
        for t, ref in enumerate((dq_ref, dk_ref, dv_ref)):
            ref[:, :half] = left[t]
            ref[:, half:] = right[t]

    roles(lambda: join(own_ref, other_ref), lambda: join(other_ref, own_ref))


def weight_kernel(g, band_ref, mine_ref, p1_ref, p2_ref, p3_ref, og_ref, og_other_ref,
                  a1_ref, a2_ref, a3_ref, b1_ref, b2_ref, b3_ref,
                  keep_ref, z1_ref, z2_ref, z3_ref, sum_s):
    line, spot_ = spot(g)
    rows = og_ref.shape[0]
    span = g * rows
    chunk = sum_s.shape[0] // g
    outer = ((og_ref, a1_ref, a2_ref, a3_ref), (og_other_ref, b1_ref, b2_ref, b3_ref))
    heads = (mine_ref, p1_ref, p2_ref, p3_ref)

    def add(pick):
        total = None
        for i in range(2):
            for d in range(g):
                part = tn(pick(i, d), outer[i][d][...])
                total = part if total is None else total + part
        sum_s[...] = total

    roles(
        lambda: add(lambda i, d: band_ref[rows_at(i * span + (spot_ ^ d) * rows, rows)]),
        lambda: add(lambda i, d: heads[d][i * rows : (i + 1) * rows]),
    )
    keep_ref[...] = sum_s[rows_at(line * chunk, chunk)]
    for d, ref in enumerate((z1_ref, z2_ref, z3_ref), 1):
        ref[...] = sum_s[rows_at((line ^ d) * chunk, chunk)].astype(BF)


def sum_kernel(keep_ref, z1_ref, z2_ref, z3_ref, out_ref):
    total = keep_ref[...]
    for ref in (z1_ref, z2_ref, z3_ref):
        total += ref[...].astype(F32)
    out_ref[...] = total.astype(BF)


def gather_kernel(g, by_line, own_ref, g1_ref, g2_ref, g3_ref, out_ref):
    line, spot_ = spot(g)
    size = own_ref.shape[0]
    at = line if by_line else spot_
    for d, ref in enumerate((own_ref, g1_ref, g2_ref, g3_ref)):
        out_ref[rows_at((at ^ d) * size, size)] = ref[...]


def body_roles(g, queries, keys, values, out_grad, out_weight, band_width, col_reach):
    q, k, v, og = queries[0], keys[0], values[0], out_grad[0]
    rows, width = q.shape
    half = width // 2
    span = g * rows
    chunk = rows // g
    devices = lax.axis_size("seq")
    both = ("dp", "seq")

    def send(value, target):
        pairs = []
        for role in range(2):
            for line in range(g):
                for place in range(g):
                    to = target(role, line, place)
                    if to is not None and 0 <= to[0] < g:
                        pairs.append((role * devices + line * g + place, role * devices + to[0] * g + to[1]))
        return lax.ppermute(value, both, pairs)

    def swap(value):
        return lax.ppermute(value, "dp", [(0, 1), (1, 0)])

    def by_role(d):
        return lambda role, line, place: (line, place ^ d) if role == 0 else (line ^ d, place)

    def along_line(d):
        return lambda role, line, place: (line ^ d, place)

    def in_group(d):
        return lambda role, line, place: (line, place ^ d)

    def second(target):
        return lambda role, line, place: target(role, line, place) if role == 1 else None

    def shift(step):
        return lambda role, line, place: (line + step, place) if role == 0 else None

    steps = range(1, g)
    og_other = swap(og)
    (to_other,) = call(pack_swap_kernel, [shaped((3, rows, half))], [q, k, v], name="pack_swap")
    other = swap(to_other)
    fields = call(functools.partial(pack_fields_kernel, g), [shaped((6 * rows, HD))] * (g - 1),
                  [q, k, v, other], name="pack_fields")
    came = [send(fields[d - 1], by_role(d)) for d in steps]
    (att,) = call(att_grad_kernel, [shaped((2, rows, half))], [og, og_other, out_weight], name="att_grad")
    fq, fkv, *back = call(
        functools.partial(forward_kernel, g),
        [shaped((2 * span, HD)), shaped((4 * span, HD))] + [shaped((4 * rows, HD))] * (g - 1)
        + [shaped((2, HS, rows, HD))],
        [col_reach, q, k, v, other, att] + came, smem=1, name="forward",
    )
    keep = back.pop()
    back = [send(back[d - 1], by_role(d)) for d in steps]
    halo = send(fkv, shift(1))
    *to_heads, mine = call(functools.partial(heads_kernel, g), [shaped((2 * rows, HD))] * g,
                           [keep] + back, name="heads")
    heads = [send(to_heads[d - 1], second(in_group(d))) for d in steps]
    near = [send(og, in_group(d)) for d in steps]
    near_other = [swap(value) for value in near]
    band_out, grads, tail = call(
        functools.partial(attention_kernel, g),
        [shaped((2 * span, HD)), shaped((2, 3, span, HD), F32), shaped((4 * span, HD))],
        [band_width, col_reach, fq, fkv, halo, att] + back, smem=2,
        scratch=[pltpu.VMEM((span, HD), BF), pltpu.VMEM((2 * span, HD), BF), pltpu.VMEM((2 * span, HD), BF),
                 pltpu.VMEM((2 * span, HD), F32), pltpu.VMEM((2 * span, HD), F32)],
        name="attention",
    )
    piece = half // g // g
    parts = call(functools.partial(weight_kernel, g),
                 [shaped((piece, width), F32)] + [shaped((piece, width))] * (g - 1),
                 [band_out, mine] + heads + [og, og_other] + near + near_other,
                 scratch=[pltpu.VMEM((half // g, width), F32)], name="weight")
    summed = [send(parts[d], along_line(d)) for d in steps]
    (piece_sum,) = call(sum_kernel, [shaped((piece, width))], [parts[0]] + summed, name="sum")
    pieces = [send(piece_sum, along_line(d)) for d in steps]
    (head_rows,) = call(functools.partial(gather_kernel, g, True), [shaped((half // g, width))],
                        [piece_sum] + pieces, name="gather_line")
    others = [send(head_rows, in_group(d)) for d in steps]
    (weight_grad,) = call(functools.partial(gather_kernel, g, False), [shaped((half, width))],
                          [head_rows] + others, name="gather_group")
    tail = send(tail, shift(-1))
    returned = call(functools.partial(pack_grads_kernel, g), [shaped((6 * rows, HD))] * g,
                    [grads, tail], name="pack_grads")
    returned = [returned[0]] + [send(returned[d], by_role(d)) for d in steps]
    own, to_other = call(functools.partial(sort_grads_kernel, g), [shaped((3, rows, half))] * 2,
                         returned, name="sort_grads")
    dq, dk, dv = call(join_grads_kernel, [shaped((rows, width))] * 3, [own, swap(to_other)], name="join_grads")
    return dq[None], dk[None], dv[None], weight_grad


def from_behind(value, axis, steps):
    count = lax.axis_size(axis)
    leading, last = (max(0, -steps), min(count, count - steps))
    return lax.ppermute(value, axis, [(source, source + steps) for source in range(leading, last)])


def attend(query_g, key_g, value_g, grad_g, allowed):
    scale = query_g.shape[-1] ** (-0.5)
    scores = jnp.einsum("gqd,gkd->gqk", query_g, key_g, preferred_element_type=F32) * scale
    scores = jnp.where(allowed, scores, -1e30)
    peak = jnp.max(scores, axis=-1, keepdims=True)
    raised = jnp.where(allowed, jnp.exp(scores - peak), 0.0)
    probs = raised / jnp.sum(raised, axis=-1, keepdims=True)
    probs_low = probs.astype(BF)
    output = jnp.einsum("gqk,gkd->gqd", probs_low, value_g, preferred_element_type=F32).astype(BF)
    delta = jnp.sum(grad_g.astype(F32) * output.astype(F32), axis=-1, keepdims=True)
    dprobs = jnp.einsum("gqd,gkd->gqk", grad_g, value_g, preferred_element_type=F32)
    dscores = (probs * (dprobs - delta)).astype(BF)
    d_query = jnp.einsum("gqk,gkd->gqd", dscores, key_g, preferred_element_type=F32) * scale
    d_key = jnp.einsum("gqk,gqd->gkd", dscores, query_g, preferred_element_type=F32) * scale
    d_value = jnp.einsum("gqk,gqd->gkd", probs_low, grad_g, preferred_element_type=F32)
    return (output, d_query, d_key, d_value)


def band_mask(q_pos, k_pos, width):
    lower = (q_pos // BLK)[None, :, None] - width[:, None, None]
    causal = k_pos[None, None, :] <= q_pos[None, :, None]
    inside = k_pos[None, None, :] >= 0
    return causal & inside & ((k_pos // BLK)[None, None, :] >= lower)


def column_mask(count, reach):
    row_q = jnp.arange(count, dtype=jnp.int32)[None, :, None]
    row_k = jnp.arange(count, dtype=jnp.int32)[None, None, :]
    return (row_k <= row_q) & (row_q - row_k < reach[:, None, None])


def column_local(field, reach, devices):
    per_dev = IMW // devices
    count = field.shape[1] // per_dev
    grid = (
        field.reshape(4, count, per_dev, HS, HD)
        .transpose(0, 2, 3, 1, 4)
        .reshape(4, per_dev * HS, count, HD)
    )
    allowed = jnp.tile(column_mask(count, reach), (per_dev, 1, 1))
    output, d_query, d_key, d_value = attend(grid[0], grid[1], grid[2], grid[3], allowed)
    stacked = jnp.stack([output, d_query.astype(BF), d_key.astype(BF), d_value.astype(BF)])
    stacked = stacked.reshape(4, per_dev, HS, count, HD).transpose(0, 3, 1, 2, 4)
    return stacked.reshape(4, count * per_dev, 1, HS, HD)


def heads_first(field, count):
    return field.reshape(count, HB, HD).transpose(1, 0, 2)


def rows_first(field, count):
    return field.transpose(1, 0, 2).reshape(count, HB * HD)


def body_any(queries, keys, values, out_grad, out_weight, band_width, col_reach):
    query_all = queries[0]
    key_all = keys[0]
    value_all = values[0]
    grad_out = out_grad[0]
    rows = query_all.shape[0]
    devices = lax.axis_size("seq")
    place = lax.axis_index("seq")
    band_dim = HB * HD
    att_grad = jnp.einsum(
        "to,ao->ta",
        grad_out,
        lax.all_gather(out_weight, "dp", axis=0, tiled=True),
        preferred_element_type=F32,
    ).astype(BF)
    strided = jnp.stack([field[:, band_dim:] for field in (query_all, key_all, value_all, att_grad)])
    strided = strided.reshape(4, rows // devices, devices, HS, HD)
    column_major = lax.all_to_all(strided, "seq", split_axis=2, concat_axis=1, tiled=True)
    column_result = column_local(column_major, col_reach, devices)
    row_major = lax.all_to_all(
        column_result, "seq", split_axis=1, concat_axis=2, tiled=True
    ).reshape(4, rows, HS * HD)
    kv_own = (key_all[:, :band_dim], value_all[:, :band_dim])
    reach_dev = -(-(WMAX * BLK) // rows)
    earlier = []
    for hop in range(reach_dev, 0, -1):
        earlier.append(from_behind((kv_own[0], kv_own[1]), "seq", hop))
    key_window = jnp.concatenate([pair[0] for pair in earlier] + [kv_own[0]], 0)
    value_window = jnp.concatenate([pair[1] for pair in earlier] + [kv_own[1]], 0)
    width_all = (reach_dev + 1) * rows
    q_pos = place * rows + jnp.arange(rows, dtype=jnp.int32)
    k_pos = (place - reach_dev) * rows + jnp.arange(width_all, dtype=jnp.int32)
    allowed = band_mask(q_pos, k_pos, band_width)
    band_out, band_dq, band_dk, band_dv = attend(
        heads_first(query_all[:, :band_dim], rows),
        heads_first(key_window, width_all),
        heads_first(value_window, width_all),
        heads_first(att_grad[:, :band_dim], rows),
        allowed,
    )
    key_rows = rows_first(band_dk, width_all)
    value_rows = rows_first(band_dv, width_all)
    key_total = key_rows[reach_dev * rows :]
    value_total = value_rows[reach_dev * rows :]
    for hop in range(1, reach_dev + 1):
        slot = (reach_dev - hop) * rows
        key_total += from_behind(key_rows[slot : slot + rows].astype(BF), "seq", -hop).astype(F32)
        value_total += from_behind(value_rows[slot : slot + rows].astype(BF), "seq", -hop).astype(F32)
    attn_out = jnp.concatenate([rows_first(band_out, rows), row_major[0]], 1)
    query_grad = jnp.concatenate([rows_first(band_dq, rows).astype(BF), row_major[1]], 1)
    key_grad = jnp.concatenate([key_total.astype(BF), row_major[2]], 1)
    value_grad = jnp.concatenate([value_total.astype(BF), row_major[3]], 1)
    shared = lax.psum_scatter(
        jnp.einsum("ta,to->ao", attn_out, grad_out, preferred_element_type=F32).astype(BF),
        "dp",
        scatter_dimension=0,
        tiled=True,
    ).astype(F32)
    weight_grad = lax.psum(shared, "seq")
    return (query_grad[None], key_grad[None], value_grad[None], weight_grad.astype(BF))


def solution(mesh):
    def body(*args):
        rows = args[0].shape[1]
        devices = mesh.shape["seq"]
        g = IMW // rows
        fits = (
            mesh.shape["dp"] == 2
            and rows == BLK
            and devices == g * g
            and g == HB == HS == 4
            and WMAX * BLK == IMW
            and args[4].shape[0] == HB * HD == HS * HD
        )
        return body_roles(g, *args) if fits else body_any(*args)

    return jax.shard_map(
        body,
        mesh=mesh,
        in_specs=(
            P("dp", "seq", None),
            P("dp", "seq", None),
            P("dp", "seq", None),
            P("dp", "seq", None),
            P("dp", None),
            P(),
            P(),
        ),
        out_specs=(P("dp", "seq", None), P("dp", "seq", None), P("dp", "seq", None), P("dp", None)),
        check_vma=False,
    )
```

```python
import functools
import math

import jax
import jax.numpy as jnp
from jax import lax
from jax.experimental import pallas as pl
from jax.experimental.pallas import tpu as pltpu
from jax.sharding import PartitionSpec as P

HD = 128
HB = 4
HS = 4
IMW = 512
BLK = 128
WMAX = 4

BF = jnp.bfloat16
F32 = jnp.float32
MIB = 1 << 20


def nn(a, b):
    return lax.dot_general(a, b, (((1,), (0,)), ((), ())), preferred_element_type=F32)


def nt(a, b):
    return lax.dot_general(a, b, (((1,), (1,)), ((), ())), preferred_element_type=F32)


def tn(a, b):
    return lax.dot_general(a, b, (((0,), (0,)), ((), ())), preferred_element_type=F32)


def rows_at(start, size):
    return pl.ds(pl.multiple_of(start, size), size)


def shaped(shape, dtype=BF):
    return jax.ShapeDtypeStruct(shape, dtype)


def call(kernel, outs, args, smem=0, left=0, left_out=False, scratch=(), mib=16, us=0.01, name=None):
    vmem = pl.BlockSpec(memory_space=pltpu.VMEM)
    anywhere = pl.BlockSpec(memory_space=pl.ANY)
    scalars = pl.BlockSpec(memory_space=pltpu.SMEM)
    return pl.pallas_call(
        kernel,
        out_shape=outs,
        in_specs=[scalars] * smem + [vmem] * (len(args) - smem - left) + [anywhere] * left,
        out_specs=[anywhere if left_out else vmem] * len(outs),
        scratch_shapes=list(scratch),
        compiler_params=pltpu.CompilerParams(vmem_limit_bytes=mib * MIB),
        cost_estimate=pl.CostEstimate(flops=0, bytes_accessed=int(us * 3.69e6), transcendentals=0),
        name=name,
    )(*args)


def roles(band, strided):
    role = lax.axis_index("dp")
    pl.when(role == 0)(band)
    pl.when(role == 1)(strided)


def spot(g):
    place = lax.axis_index("seq")
    return lax.div(place, g), lax.rem(place, g)


def read_field(own_ref, other_ref, att_ref, i, t):
    if t == 3:
        return lambda rows, lanes: att_ref[i, rows, lanes]
    return lambda rows, lanes: (own_ref, other_ref)[i][t, rows, lanes]


def pack_fields_kernel(g, own_ref, other_ref, att_ref, *out_refs):
    line, spot_ = spot(g)
    rows = own_ref.shape[1]
    chunk = rows // g
    fields = [(i, t, read_field(own_ref, other_ref, att_ref, i, t)) for i in range(2) for t in range(4)]

    def band():
        for d in range(1, g):
            for i, t, read in fields:
                at = (i * 4 + t) * rows
                out_refs[d - 1][at : at + rows] = read(slice(None), rows_at((spot_ ^ d) * HD, HD))

    def strided():
        for d in range(1, g):
            there = rows_at((line ^ d) * chunk, chunk)
            for i, t, read in fields:
                for h in range(HS):
                    at = (i * 4 + t) * rows + h * chunk
                    out_refs[d - 1][at : at + chunk] = read(there, slice(h * HD, (h + 1) * HD))

    roles(band, strided)


def att_grad_kernel(own_ref, other_ref, weight_ref, out_ref):
    out_ref[0] = nt(own_ref[...], weight_ref[...]).astype(BF)
    out_ref[1] = nt(other_ref[...], weight_ref[...]).astype(BF)


def strided_bias(rows, chunk, reach):
    key = lax.broadcasted_iota(jnp.int32, (rows, rows), 0)
    query = lax.broadcasted_iota(jnp.int32, (rows, rows), 1)
    apart = lax.div(query, chunk) - lax.div(key, chunk)
    same = lax.rem(key, chunk) == lax.rem(query, chunk)
    return jnp.where(same & (apart >= 0) & (apart < reach), 0.0, -1e30)


def score_grads(probs, probs_low, dprobs):
    delta = jnp.sum(probs_low.astype(F32) * dprobs, axis=0, keepdims=True)
    return (probs * (dprobs - delta)).astype(BF), delta


SCALE = HD ** (-0.5)
SCALE_2 = SCALE / math.log(2)


def softmax(scores, bias):
    scores = scores * SCALE_2 + bias
    peak = jnp.max(scores, axis=0, keepdims=True)
    raised = jnp.exp2(scores - peak)
    total = jnp.sum(raised, axis=0, keepdims=True)
    return raised * (1.0 / total), peak + jnp.log2(total)


def forward_kernel(g, reach_ref, own_ref, other_ref, att_ref, r1_ref, r2_ref, r3_ref,
                   fqg_ref, fkv_ref, o1_ref, o2_ref, o3_ref, keep_ref, grads_ref):
    line, spot_ = spot(g)
    rows = own_ref.shape[1]
    span = g * rows
    chunk = rows // g
    came = (r1_ref, r2_ref, r3_ref)
    back = (o1_ref, o2_ref, o3_ref)
    fields = [(i, t, read_field(own_ref, other_ref, att_ref, i, t)) for i in range(2) for t in range(4)]

    def put(i, t, start, size, value):
        ref = (fqg_ref, fkv_ref, fkv_ref, fqg_ref)[t]
        ref[rows_at((t // 2 * 2 + i) * span + start, size)] = value

    def band():
        for i, t, read in fields:
            at = (i * 4 + t) * rows
            put(i, t, spot_ * rows, rows, read(slice(None), rows_at(spot_ * HD, HD)))
            for d in range(1, g):
                put(i, t, (spot_ ^ d) * rows, rows, came[d - 1][at : at + rows])

    def strided():
        here = rows_at(line * chunk, chunk)
        for i, t, read in fields:
            for h in range(HS):
                at = (i * 4 + t) * rows + h * chunk
                put(i, t, h * rows + line * chunk, chunk, read(here, slice(h * HD, (h + 1) * HD)))
                for d in range(1, g):
                    put(i, t, h * rows + (line ^ d) * chunk, chunk, came[d - 1][at : at + chunk])
        each = [(i, h) for h in range(HS) for i in range(2)]

        def head(t, i, h):
            at = (t // 2 * 2 + i) * span + h * rows
            return (fqg_ref, fkv_ref, fkv_ref, fqg_ref)[t][at : at + rows]

        scores, dprobs, probs = {}, {}, {}
        for i, h in each:
            scores[i, h] = nt(head(1, i, h), head(0, i, h))
            dprobs[i, h] = nt(head(2, i, h), head(3, i, h))
        for h in range(HS):
            bias = strided_bias(rows, chunk, reach_ref[h])
            for i in range(2):
                probs[i, h], _ = softmax(scores[i, h], bias)
        for i, h in each:
            keep_ref[i, h] = tn(probs[i, h].astype(BF), head(2, i, h)).astype(BF)
        for d in range(1, g):
            there = rows_at((line ^ d) * chunk, chunk)
            for i, h in each:
                at = (i * HS + h) * chunk
                back[d - 1][at : at + chunk] = keep_ref[i, h, there]
        for i, h in each:
            mine = slice(h * rows, (h + 1) * rows)
            probs_low = probs[i, h].astype(BF)
            dscores, _ = score_grads(probs[i, h], probs_low, dprobs[i, h])
            grads_ref[i, 0, mine] = (tn(dscores, head(1, i, h)) * SCALE).astype(BF)
            grads_ref[i, 1, mine] = (nn(dscores, head(0, i, h)) * SCALE).astype(BF)
            grads_ref[i, 2, mine] = nn(probs_low, head(3, i, h)).astype(BF)

    roles(band, strided)


def heads_kernel(g, keep_ref, o1_ref, o2_ref, o3_ref, p1_ref, p2_ref, p3_ref, mine_ref):
    line, spot_ = spot(g)
    rows = keep_ref.shape[2]
    chunk = rows // g
    came = (o1_ref, o2_ref, o3_ref)
    outs = (mine_ref, p1_ref, p2_ref, p3_ref)

    def strided():
        for to in range(g):
            head = spot_ ^ to
            for i in range(2):
                outs[to][rows_at(i * rows + line * chunk, chunk)] = keep_ref[i, head, rows_at(line * chunk, chunk)]
                for d in range(1, g):
                    source = rows_at((i * HS + head) * chunk, chunk)
                    outs[to][rows_at(i * rows + (line ^ d) * chunk, chunk)] = came[d - 1][source]

    roles(lambda: None, strided)


def attention_kernel(g, width_ref, fqg_ref, fkv_ref, halo_ref, order_ref,
                     out_ref, dquery_ref, dkv_ref, stats_ref, key_s, value_s, key_t, value_t):
    line, spot_ = spot(g)
    span = dquery_ref.shape[1]
    rows = span // g

    def band():
        width = width_ref[spot_]
        key_at = lax.broadcasted_iota(jnp.int32, (span + rows, rows), 0)
        query_at = lax.broadcasted_iota(jnp.int32, (span + rows, rows), 1)
        block = lax.div(key_at, BLK)
        near = (block >= WMAX - width) & (key_at - span <= query_at)
        for i in range(2):
            for t, ref in enumerate((key_s, value_s)):
                here = slice((t * 2 + i) * span, (t * 2 + i + 1) * span)
                ref[i, :span] = halo_ref[here]
                ref[i, span:] = fkv_ref[here]
            key_t[i] = key_s[i].T
            value_t[i] = value_s[i].T
        for b in reversed(range(g)):
            bias = jnp.where(near & ((block + b >= g) | (line > 0)), 0.0, -1e30)
            window = slice(b * rows, b * rows + span + rows)
            mine = slice(b * rows, (b + 1) * rows)
            own = slice(span - b * rows, span + rows)
            for i in range(2):
                query = fqg_ref[i * span + b * rows : i * span + (b + 1) * rows]
                grad = fqg_ref[(2 + i) * span + b * rows : (2 + i) * span + (b + 1) * rows]
                probs, total = softmax(nt(key_s[i, window], query), bias)
                probs_low = probs.astype(BF)
                out_ref[i, :, mine] = nn(value_t[i, :, window], probs_low).astype(BF)
                dscores, delta = score_grads(probs, probs_low, nt(value_s[i, window], grad))
                stats_ref[i * 8 : i * 8 + 1, mine] = total
                stats_ref[i * 8 + 1 : i * 8 + 2, mine] = delta
                dquery_ref[i, mine] = (nn(key_t[i, :, window], dscores) * SCALE).astype(BF).T
                dkey = nn(dscores[own], query) * SCALE
                dvalue = nn(probs_low[own], grad)
                if b == g - 1:
                    dkv_ref[i, 0] = dkey
                    dkv_ref[i, 1] = dvalue
                else:
                    dkv_ref[i, 0, : (b + 1) * rows] += dkey
                    dkv_ref[i, 1, : (b + 1) * rows] += dvalue

    roles(band, lambda: None)


def tail_kernel(g, width_ref, fkv_ref, next_ref, stats_ref, dkv_ref, out_ref):
    line, spot_ = spot(g)
    span = dkv_ref.shape[2]
    rows = span // g

    def band():
        out_ref[...] = dkv_ref[...]

        @pl.when(line < g - 1)
        def _():
            width = width_ref[spot_]
            for b in range(g):
                block = lax.div(lax.broadcasted_iota(jnp.int32, (span - b * rows, rows), 0), BLK)
                bias = jnp.where(block >= WMAX - width, 0.0, -1e30)
                mine = slice(b * rows, (b + 1) * rows)
                for i in range(2):
                    query = next_ref[i * span + b * rows : i * span + (b + 1) * rows]
                    grad = next_ref[(2 + i) * span + b * rows : (2 + i) * span + (b + 1) * rows]
                    key = fkv_ref[i * span + b * rows : (i + 1) * span]
                    value = fkv_ref[(2 + i) * span + b * rows : (3 + i) * span]
                    total = stats_ref[i * 8 : i * 8 + 1, mine]
                    delta = stats_ref[i * 8 + 1 : i * 8 + 2, mine]
                    probs = jnp.exp2(nt(key, query) * SCALE_2 + bias - total)
                    dscores = (probs * (nt(value, grad) - delta)).astype(BF)
                    out_ref[i, 0, b * rows :] += nn(dscores, query) * SCALE
                    out_ref[i, 1, b * rows :] += nn(probs.astype(BF), grad)

    roles(band, lambda: None)


def weight_kernel(g, out_ref, mine_ref, p1_ref, p2_ref, p3_ref, og_ref, og_other_ref,
                  a1_ref, a2_ref, a3_ref, b1_ref, b2_ref, b3_ref, part_ref, z1_ref, z2_ref, z3_ref, sum_s):
    line, spot_ = spot(g)
    rows = og_ref.shape[0]
    chunk = rows // g
    heads = (mine_ref, p1_ref, p2_ref, p3_ref)

    outer = ((og_ref, a1_ref, a2_ref, a3_ref), (og_other_ref, b1_ref, b2_ref, b3_ref))

    def add(part):
        sum_s[...] = sum(part(i, d) for i in range(2) for d in range(g))

    roles(
        lambda: add(lambda i, d: nn(out_ref[i, :, rows_at((spot_ ^ d) * rows, rows)], outer[i][d][...])),
        lambda: add(lambda i, d: tn(heads[d][i * rows : (i + 1) * rows], outer[i][d][...])),
    )
    part_ref[...] = sum_s[rows_at(line * chunk, chunk)]
    for d, ref in enumerate((z1_ref, z2_ref, z3_ref), 1):
        ref[...] = sum_s[rows_at((line ^ d) * chunk, chunk)].astype(BF)


def pack_grads_kernel(g, dquery_ref, dkv_ref, strided_ref, keep_ref, r1_ref, r2_ref, r3_ref):
    line, spot_ = spot(g)
    span = dquery_ref.shape[1]
    rows = span // g
    chunk = rows // g
    outs = (keep_ref, r1_ref, r2_ref, r3_ref)

    def band():
        for d in range(g):
            block = rows_at((spot_ ^ d) * rows, rows)
            for i in range(2):
                for t in range(3):
                    value = dquery_ref[i, block] if t == 0 else dkv_ref[i, t - 1, block].astype(BF)
                    outs[d][(i * 3 + t) * rows : (i * 3 + t + 1) * rows] = value

    def strided():
        for d in range(g):
            for i in range(2):
                for t in range(3):
                    for h in range(HS):
                        at = (i * 3 + t) * rows + h * chunk
                        there = rows_at(h * rows + (line ^ d) * chunk, chunk)
                        outs[d][at : at + chunk] = strided_ref[i, t, there]

    roles(band, strided)


def sort_grads_kernel(g, keep_ref, r1_ref, r2_ref, r3_ref, own_ref, *rest):
    line, spot_ = spot(g)
    rows = own_ref.shape[1]
    chunk = rows // g
    came = (keep_ref, r1_ref, r2_ref, r3_ref)
    piece_refs, other_s = rest[:-1], rest[-1]

    def band():
        for d in range(g):
            lanes = rows_at((spot_ ^ d) * HD, HD)
            for t in range(3):
                own_ref[t, :, lanes] = came[d][t * rows : (t + 1) * rows]
                other_s[t * rows : (t + 1) * rows, lanes] = came[d][(3 + t) * rows : (4 + t) * rows]

    def strided():
        for d in range(g):
            for t in range(3):
                for h in range(HS):
                    lanes = slice(h * HD, (h + 1) * HD)
                    at = t * rows + h * chunk
                    own_ref[t, rows_at((line ^ d) * chunk, chunk), lanes] = came[d][at : at + chunk]
                    there = rows_at(t * rows + (line ^ d) * chunk, chunk)
                    other_s[there, lanes] = came[d][3 * rows + at : 3 * rows + at + chunk]

    roles(band, strided)
    for n, ref in enumerate(piece_refs):
        ref[...] = other_s[n * ref.shape[0] : (n + 1) * ref.shape[0]]


def sum_kernel(keep_ref, z1_ref, z2_ref, z3_ref, out_ref):
    total = keep_ref[...]
    for ref in (z1_ref, z2_ref, z3_ref):
        total += ref[...].astype(F32)
    out_ref[...] = total.astype(BF)


def gather_kernel(g, own_ref, g1_ref, g2_ref, g3_ref, out_ref):
    line, _ = spot(g)
    size = own_ref.shape[0]
    for d, ref in enumerate((own_ref, g1_ref, g2_ref, g3_ref)):
        out_ref[rows_at((line ^ d) * size, size)] = ref[...]


def finish_kernel(g, own_ref, b0_ref, b1_ref, b2_ref, b3_ref, r0_ref, r1_ref, r2_ref, r3_ref,
                  dq_ref, dk_ref, dv_ref, weight_ref, sems):
    _, spot_ = spot(g)
    rows, half = own_ref.shape[1:]
    size = r0_ref.shape[0]
    pieces = (b0_ref, b1_ref, b2_ref, b3_ref)
    outs = (dq_ref, dk_ref, dv_ref)
    piece = b0_ref.shape[0]

    def run(own_at, other_at):
        copies = [
            (ref, weight_ref.at[rows_at((spot_ ^ d) * size, size)])
            for d, ref in enumerate((r0_ref, r1_ref, r2_ref, r3_ref))
        ]
        for t in range(3):
            copies.append((own_ref.at[t], outs[t].at[:, pl.ds(own_at, half)]))
        for n in range(4):
            start, stop = n * piece, (n + 1) * piece
            while start < stop:
                t = start // rows
                size_ = min(stop, (t + 1) * rows) - start
                copies.append((pieces[n].at[pl.ds(start - n * piece, size_)],
                               outs[t].at[pl.ds(start - t * rows, size_), pl.ds(other_at, half)]))
                start += size_
        copies = [pltpu.make_async_copy(src, dst, sems.at[n]) for n, (src, dst) in enumerate(copies)]
        for copy in copies:
            copy.start()
        for copy in copies:
            copy.wait()

    roles(lambda: run(0, half), lambda: run(half, 0))


def body_roles(g, queries, keys, values, out_grad, out_weight, band_width, col_reach):
    q, k, v, og = queries[0], keys[0], values[0], out_grad[0]
    rows, width = q.shape
    half = width // 2
    span = g * rows
    chunk = rows // g
    devices = lax.axis_size("seq")
    both = ("dp", "seq")

    def send(value, target):
        pairs = []
        for role in range(2):
            for line in range(g):
                for place in range(g):
                    to = target(role, line, place)
                    if to is None:
                        continue
                    to_role, to_line, to_place = to
                    pairs.append((role * devices + line * g + place, to_role * devices + to_line * g + to_place))
        return lax.ppermute(value, both, pairs)

    def swap(value):
        return lax.ppermute(value, "dp", [(0, 1), (1, 0)])

    def by_role(d):
        return lambda role, line, place: (0, line, place ^ d) if role == 0 else (1, line ^ d, place)

    def along_line(d):
        return lambda role, line, place: (role, line ^ d, place)

    def in_group(d):
        return lambda role, line, place: (role, line, place ^ d)

    def shift(step):
        return lambda role, line, place: (0, line + step, place) if role == 0 and 0 <= line + step < g else None

    def ring(step):
        def target(role, line, place):
            to = line + (step if role == 0 else -step)
            return (role, to, place) if 0 <= to < g else (1 - role, line, place)

        return target

    steps = range(1, g)
    role = lax.axis_index("dp")
    og_other = swap(og)
    to_other = jnp.stack([lax.dynamic_slice(value, (0, (1 - role) * half), (rows, half)) for value in (q, k, v)])
    own = jnp.stack([lax.dynamic_slice(value, (0, role * half), (rows, half)) for value in (q, k, v)])
    other = swap(to_other)
    (att,) = call(att_grad_kernel, [shaped((2, rows, half))], [og, og_other, out_weight], name="att_grad")
    packed = call(functools.partial(pack_fields_kernel, g), [shaped((8 * rows, HD))] * (g - 1),
                  [own, other, att], name="pack_fields")
    came = [send(packed[d - 1], by_role(d)) for d in steps]
    near = [send(og, in_group(d)) for d in steps]
    near_other = [swap(value) for value in near]
    fqg, fkv, *back, keep, strided_grads = call(
        functools.partial(forward_kernel, g),
        [shaped((4 * span, HD))] * 2 + [shaped((2 * rows, HD))] * (g - 1)
        + [shaped((2, HS, rows, HD)), shaped((2, 3, span, HD))],
        [col_reach, own, other, att] + came, smem=1, name="forward",
    )
    halo = send(fkv, shift(1))
    following = send(fqg, shift(-1))
    back = [send(back[d - 1], by_role(d)) for d in steps]
    *to_heads, mine = call(functools.partial(heads_kernel, g), [shaped((2 * rows, HD))] * g,
                           [keep] + back, name="heads")
    heads = [send(to_heads[d - 1], in_group(d)) for d in steps]
    band_out, dquery, dkv, stats = call(
        functools.partial(attention_kernel, g),
        [shaped((2, HD, span)), shaped((2, span, HD)), shaped((2, 2, span, HD), F32), shaped((16, span), F32)],
        [band_width, fqg, fkv, halo, following], smem=1, left=1,
        scratch=[pltpu.VMEM((2, 2 * span, HD), BF), pltpu.VMEM((2, 2 * span, HD), BF),
                 pltpu.VMEM((2, HD, 2 * span), BF), pltpu.VMEM((2, HD, 2 * span), BF)],
        mib=24, name="attention",
    )
    piece = half // g // g
    parts = call(
        functools.partial(weight_kernel, g), [shaped((piece, width), F32)] + [shaped((piece, width))] * (g - 1),
        [band_out, mine] + heads + [og, og_other] + near + near_other,
        scratch=[pltpu.VMEM((half // g, width), F32)], name="weight",
    )
    summed = [send(parts[d], along_line(d)) for d in steps]
    stats = send(stats, ring(-1))
    (dkv,) = call(functools.partial(tail_kernel, g), [shaped(dkv.shape, F32)],
                  [band_width, fkv, following, stats, dkv], smem=1, name="tail")
    (piece_sum,) = call(sum_kernel, [shaped((piece, width))], [parts[0]] + summed, name="sum")
    pieces = [send(piece_sum, along_line(d)) for d in steps]
    (head_rows,) = call(functools.partial(gather_kernel, g), [shaped((half // g, width))],
                        [piece_sum] + pieces, name="gather_line")
    others = [send(head_rows, in_group(d)) for d in steps]
    returned = call(functools.partial(pack_grads_kernel, g), [shaped((6 * rows, HD))] * g,
                    [dquery, dkv, strided_grads], name="pack_grads")
    returned = [returned[0]] + [send(returned[d], by_role(d)) for d in steps]
    own, *to_other = call(functools.partial(sort_grads_kernel, g),
                          [shaped((3, rows, half))] + [shaped((3 * rows // 4, half))] * 4, returned,
                          scratch=[pltpu.VMEM((3 * rows, half), BF)], name="sort_grads")
    dq, dk, dv, weight_grad = call(
        functools.partial(finish_kernel, g), [shaped((rows, width))] * 3 + [shaped((half, width))],
        [own] + [swap(value) for value in to_other] + [head_rows] + others, left_out=True,
        scratch=[pltpu.SemaphoreType.DMA((g + 12,))], name="finish",
    )
    return dq[None], dk[None], dv[None], weight_grad


def from_behind(value, axis, steps):
    count = lax.axis_size(axis)
    leading, last = (max(0, -steps), min(count, count - steps))
    return lax.ppermute(value, axis, [(source, source + steps) for source in range(leading, last)])


def attend(query_g, key_g, value_g, grad_g, allowed):
    scale = query_g.shape[-1] ** (-0.5)
    scores = jnp.einsum("gqd,gkd->gqk", query_g, key_g, preferred_element_type=F32) * scale
    scores = jnp.where(allowed, scores, -1e30)
    peak = jnp.max(scores, axis=-1, keepdims=True)
    raised = jnp.where(allowed, jnp.exp(scores - peak), 0.0)
    probs = raised / jnp.sum(raised, axis=-1, keepdims=True)
    probs_low = probs.astype(BF)
    output = jnp.einsum("gqk,gkd->gqd", probs_low, value_g, preferred_element_type=F32).astype(BF)
    delta = jnp.sum(grad_g.astype(F32) * output.astype(F32), axis=-1, keepdims=True)
    dprobs = jnp.einsum("gqd,gkd->gqk", grad_g, value_g, preferred_element_type=F32)
    dscores = (probs * (dprobs - delta)).astype(BF)
    d_query = jnp.einsum("gqk,gkd->gqd", dscores, key_g, preferred_element_type=F32) * scale
    d_key = jnp.einsum("gqk,gqd->gkd", dscores, query_g, preferred_element_type=F32) * scale
    d_value = jnp.einsum("gqk,gqd->gkd", probs_low, grad_g, preferred_element_type=F32)
    return (output, d_query, d_key, d_value)


def band_mask(q_pos, k_pos, width):
    lower = (q_pos // BLK)[None, :, None] - width[:, None, None]
    causal = k_pos[None, None, :] <= q_pos[None, :, None]
    inside = k_pos[None, None, :] >= 0
    return causal & inside & ((k_pos // BLK)[None, None, :] >= lower)


def column_mask(count, reach):
    row_q = jnp.arange(count, dtype=jnp.int32)[None, :, None]
    row_k = jnp.arange(count, dtype=jnp.int32)[None, None, :]
    return (row_k <= row_q) & (row_q - row_k < reach[:, None, None])


def column_local(field, reach, devices):
    per_dev = IMW // devices
    count = field.shape[1] // per_dev
    grid = (
        field.reshape(4, count, per_dev, HS, HD)
        .transpose(0, 2, 3, 1, 4)
        .reshape(4, per_dev * HS, count, HD)
    )
    allowed = jnp.tile(column_mask(count, reach), (per_dev, 1, 1))
    output, d_query, d_key, d_value = attend(grid[0], grid[1], grid[2], grid[3], allowed)
    stacked = jnp.stack([output, d_query.astype(BF), d_key.astype(BF), d_value.astype(BF)])
    stacked = stacked.reshape(4, per_dev, HS, count, HD).transpose(0, 3, 1, 2, 4)
    return stacked.reshape(4, count * per_dev, 1, HS, HD)


def heads_first(field, count):
    return field.reshape(count, HB, HD).transpose(1, 0, 2)


def rows_first(field, count):
    return field.transpose(1, 0, 2).reshape(count, HB * HD)


def body_any(queries, keys, values, out_grad, out_weight, band_width, col_reach):
    query_all = queries[0]
    key_all = keys[0]
    value_all = values[0]
    grad_out = out_grad[0]
    rows = query_all.shape[0]
    devices = lax.axis_size("seq")
    place = lax.axis_index("seq")
    band_dim = HB * HD
    att_grad = jnp.einsum(
        "to,ao->ta",
        grad_out,
        lax.all_gather(out_weight, "dp", axis=0, tiled=True),
        preferred_element_type=F32,
    ).astype(BF)
    strided = jnp.stack([field[:, band_dim:] for field in (query_all, key_all, value_all, att_grad)])
    strided = strided.reshape(4, rows // devices, devices, HS, HD)
    column_major = lax.all_to_all(strided, "seq", split_axis=2, concat_axis=1, tiled=True)
    column_result = column_local(column_major, col_reach, devices)
    row_major = lax.all_to_all(
        column_result, "seq", split_axis=1, concat_axis=2, tiled=True
    ).reshape(4, rows, HS * HD)
    kv_own = (key_all[:, :band_dim], value_all[:, :band_dim])
    reach_dev = -(-(WMAX * BLK) // rows)
    earlier = []
    for hop in range(reach_dev, 0, -1):
        earlier.append(from_behind((kv_own[0], kv_own[1]), "seq", hop))
    key_window = jnp.concatenate([pair[0] for pair in earlier] + [kv_own[0]], 0)
    value_window = jnp.concatenate([pair[1] for pair in earlier] + [kv_own[1]], 0)
    width_all = (reach_dev + 1) * rows
    q_pos = place * rows + jnp.arange(rows, dtype=jnp.int32)
    k_pos = (place - reach_dev) * rows + jnp.arange(width_all, dtype=jnp.int32)
    allowed = band_mask(q_pos, k_pos, band_width)
    band_out, band_dq, band_dk, band_dv = attend(
        heads_first(query_all[:, :band_dim], rows),
        heads_first(key_window, width_all),
        heads_first(value_window, width_all),
        heads_first(att_grad[:, :band_dim], rows),
        allowed,
    )
    key_rows = rows_first(band_dk, width_all)
    value_rows = rows_first(band_dv, width_all)
    key_total = key_rows[reach_dev * rows :]
    value_total = value_rows[reach_dev * rows :]
    for hop in range(1, reach_dev + 1):
        slot = (reach_dev - hop) * rows
        key_total += from_behind(key_rows[slot : slot + rows].astype(BF), "seq", -hop).astype(F32)
        value_total += from_behind(value_rows[slot : slot + rows].astype(BF), "seq", -hop).astype(F32)
    attn_out = jnp.concatenate([rows_first(band_out, rows), row_major[0]], 1)
    query_grad = jnp.concatenate([rows_first(band_dq, rows).astype(BF), row_major[1]], 1)
    key_grad = jnp.concatenate([key_total.astype(BF), row_major[2]], 1)
    value_grad = jnp.concatenate([value_total.astype(BF), row_major[3]], 1)
    shared = lax.psum_scatter(
        jnp.einsum("ta,to->ao", attn_out, grad_out, preferred_element_type=F32).astype(BF),
        "dp",
        scatter_dimension=0,
        tiled=True,
    ).astype(F32)
    weight_grad = lax.psum(shared, "seq")
    return (query_grad[None], key_grad[None], value_grad[None], weight_grad.astype(BF))


def solution(mesh):
    def body(*args):
        rows = args[0].shape[1]
        devices = mesh.shape["seq"]
        g = IMW // rows
        fits = (
            mesh.shape["dp"] == 2
            and rows == BLK
            and devices == g * g
            and g == HB == HS == 4
            and WMAX * BLK == IMW
            and args[4].shape[0] == HB * HD == HS * HD
        )
        return body_roles(g, *args) if fits else body_any(*args)

    return jax.shard_map(
        body,
        mesh=mesh,
        in_specs=(
            P("dp", "seq", None),
            P("dp", "seq", None),
            P("dp", "seq", None),
            P("dp", "seq", None),
            P("dp", None),
            P(),
            P(),
        ),
        out_specs=(P("dp", "seq", None), P("dp", "seq", None), P("dp", "seq", None), P("dp", None)),
        check_vma=False,
    )
```

```python
import functools
import math

import jax
import jax.numpy as jnp
from jax import lax
from jax.experimental import pallas as pl
from jax.experimental.pallas import tpu as pltpu
from jax.sharding import PartitionSpec as P

HD = 128
HB = 4
HS = 4
IMW = 512
BLK = 128
WMAX = 4

BF = jnp.bfloat16
F32 = jnp.float32
MIB = 1 << 20


def nn(a, b):
    return lax.dot_general(a, b, (((1,), (0,)), ((), ())), preferred_element_type=F32)


def nt(a, b):
    return lax.dot_general(a, b, (((1,), (1,)), ((), ())), preferred_element_type=F32)


def tn(a, b):
    return lax.dot_general(a, b, (((0,), (0,)), ((), ())), preferred_element_type=F32)


def rows_at(start, size):
    return pl.ds(pl.multiple_of(start, size), size)


def shaped(shape, dtype=BF):
    return jax.ShapeDtypeStruct(shape, dtype)


def call(kernel, outs, args, smem=0, left_out=False, order=(), scratch=(), mib=16, name=None):
    vmem = pl.BlockSpec(memory_space=pltpu.VMEM)
    scalars = pl.BlockSpec(memory_space=pltpu.SMEM)
    anywhere = pl.BlockSpec(memory_space=pl.ANY)
    count = len(args)

    def body(*refs):
        kernel(*refs[:count], *refs[count + len(order) :])

    return pl.pallas_call(
        body,
        out_shape=outs,
        in_specs=[scalars] * smem + [vmem] * (count - smem) + [anywhere] * len(order),
        out_specs=[anywhere if left_out else vmem] * len(outs),
        scratch_shapes=list(scratch),
        compiler_params=pltpu.CompilerParams(vmem_limit_bytes=mib * MIB),
        name=name,
    )(*args, *order)


def roles(band, strided):
    role = lax.axis_index("dp")
    pl.when(role == 0)(band)
    pl.when(role == 1)(strided)


def spot(g):
    place = lax.axis_index("seq")
    return lax.div(place, g), lax.rem(place, g)


def read_field(own_ref, other_ref, att_ref, i, t):
    if t == 3:
        return lambda rows, lanes: att_ref[i, rows, lanes]
    return lambda rows, lanes: (own_ref, other_ref)[i][t, rows, lanes]


def pack_fields_kernel(g, own_ref, other_ref, att_ref, *out_refs):
    line, spot_ = spot(g)
    rows = own_ref.shape[1]
    chunk = rows // g
    fields = [(i, t, read_field(own_ref, other_ref, att_ref, i, t)) for i in range(2) for t in range(4)]

    def band():
        for d in range(1, g):
            for i, t, read in fields:
                at = (i * 4 + t) * rows
                out_refs[d - 1][at : at + rows] = read(slice(None), rows_at((spot_ ^ d) * HD, HD))

    def strided():
        for d in range(1, g):
            there = rows_at((line ^ d) * chunk, chunk)
            for i, t, read in fields:
                for h in range(HS):
                    at = (i * 4 + t) * rows + h * chunk
                    out_refs[d - 1][at : at + chunk] = read(there, slice(h * HD, (h + 1) * HD))

    roles(band, strided)


def att_grad_kernel(own_ref, other_ref, weight_ref, out_ref):
    out_ref[0] = nt(own_ref[...], weight_ref[...]).astype(BF)
    out_ref[1] = nt(other_ref[...], weight_ref[...]).astype(BF)


def strided_bias(rows, chunk, reach):
    key = lax.broadcasted_iota(jnp.int32, (rows, rows), 0)
    query = lax.broadcasted_iota(jnp.int32, (rows, rows), 1)
    apart = lax.div(query, chunk) - lax.div(key, chunk)
    same = lax.rem(key, chunk) == lax.rem(query, chunk)
    return jnp.where(same & (apart >= 0) & (apart < reach), 0.0, -1e30)


def score_grads(probs, probs_low, dprobs):
    delta = jnp.sum(probs_low.astype(F32) * dprobs, axis=0, keepdims=True)
    return (probs * (dprobs - delta)).astype(BF), delta


SCALE = HD ** (-0.5)
SCALE_2 = SCALE / math.log(2)


def softmax(scores, bias):
    scores = scores * SCALE_2 + bias
    peak = jnp.max(scores, axis=0, keepdims=True)
    raised = jnp.exp2(scores - peak)
    total = jnp.sum(raised, axis=0, keepdims=True)
    return raised * (1.0 / total), peak + jnp.log2(total)


def forward_kernel(g, reach_ref, own_ref, other_ref, att_ref, r1_ref, r2_ref, r3_ref,
                   fqg_ref, fkv_ref, o1_ref, o2_ref, o3_ref, keep_ref, grads_ref):
    line, spot_ = spot(g)
    rows = own_ref.shape[1]
    span = g * rows
    chunk = rows // g
    came = (r1_ref, r2_ref, r3_ref)
    back = (o1_ref, o2_ref, o3_ref)
    fields = [(i, t, read_field(own_ref, other_ref, att_ref, i, t)) for i in range(2) for t in range(4)]

    def put(i, t, start, size, value):
        ref = (fqg_ref, fkv_ref, fkv_ref, fqg_ref)[t]
        ref[rows_at((t // 2 * 2 + i) * span + start, size)] = value

    def band():
        for i, t, read in fields:
            at = (i * 4 + t) * rows
            put(i, t, spot_ * rows, rows, read(slice(None), rows_at(spot_ * HD, HD)))
            for d in range(1, g):
                put(i, t, (spot_ ^ d) * rows, rows, came[d - 1][at : at + rows])

    def strided():
        here = rows_at(line * chunk, chunk)
        for i, t, read in fields:
            for h in range(HS):
                at = (i * 4 + t) * rows + h * chunk
                put(i, t, h * rows + line * chunk, chunk, read(here, slice(h * HD, (h + 1) * HD)))
                for d in range(1, g):
                    put(i, t, h * rows + (line ^ d) * chunk, chunk, came[d - 1][at : at + chunk])
        each = [(i, h) for h in range(HS) for i in range(2)]

        def head(t, i, h):
            at = (t // 2 * 2 + i) * span + h * rows
            return (fqg_ref, fkv_ref, fkv_ref, fqg_ref)[t][at : at + rows]

        scores, dprobs, probs = {}, {}, {}
        for i, h in each:
            scores[i, h] = nt(head(1, i, h), head(0, i, h))
            dprobs[i, h] = nt(head(2, i, h), head(3, i, h))
        for h in range(HS):
            bias = strided_bias(rows, chunk, reach_ref[h])
            for i in range(2):
                probs[i, h], _ = softmax(scores[i, h], bias)
        for i, h in each:
            keep_ref[i, h] = tn(probs[i, h].astype(BF), head(2, i, h)).astype(BF)
        for d in range(1, g):
            there = rows_at((line ^ d) * chunk, chunk)
            for i, h in each:
                at = (i * HS + h) * chunk
                back[d - 1][at : at + chunk] = keep_ref[i, h, there]
        for i, h in each:
            mine = slice(h * rows, (h + 1) * rows)
            probs_low = probs[i, h].astype(BF)
            dscores, _ = score_grads(probs[i, h], probs_low, dprobs[i, h])
            grads_ref[i, 0, mine] = (tn(dscores, head(1, i, h)) * SCALE).astype(BF)
            grads_ref[i, 1, mine] = (nn(dscores, head(0, i, h)) * SCALE).astype(BF)
            grads_ref[i, 2, mine] = nn(probs_low, head(3, i, h)).astype(BF)

    roles(band, strided)


def heads_kernel(g, keep_ref, o1_ref, o2_ref, o3_ref, p1_ref, p2_ref, p3_ref, mine_ref):
    line, spot_ = spot(g)
    rows = keep_ref.shape[2]
    chunk = rows // g
    came = (o1_ref, o2_ref, o3_ref)
    outs = (mine_ref, p1_ref, p2_ref, p3_ref)

    def strided():
        for to in range(g):
            head = spot_ ^ to
            for i in range(2):
                outs[to][rows_at(i * rows + line * chunk, chunk)] = keep_ref[i, head, rows_at(line * chunk, chunk)]
                for d in range(1, g):
                    source = rows_at((i * HS + head) * chunk, chunk)
                    outs[to][rows_at(i * rows + (line ^ d) * chunk, chunk)] = came[d - 1][source]

    roles(lambda: None, strided)


def attention_kernel(g, width_ref, fqg_ref, fkv_ref, halo_ref,
                     out_ref, dquery_ref, dkv_ref, stats_ref, key_s, value_s, key_t, value_t):
    line, spot_ = spot(g)
    span = dquery_ref.shape[1]
    rows = span // g

    def band():
        width = width_ref[spot_]
        key_at = lax.broadcasted_iota(jnp.int32, (span + rows, rows), 0)
        query_at = lax.broadcasted_iota(jnp.int32, (span + rows, rows), 1)
        block = lax.div(key_at, BLK)
        near = (block >= WMAX - width) & (key_at - span <= query_at)
        for i in range(2):
            for t, ref in enumerate((key_s, value_s)):
                at = (t * 2 + i) * span
                ref[i, span:] = fkv_ref[at : at + span]
                ref[i, :span] = halo_ref[at : at + span]
            key_t[i] = key_s[i].T
            value_t[i] = value_s[i].T
        for b in reversed(range(g)):
            bias = jnp.where(near & ((block + b >= g) | (line > 0)), 0.0, -1e30)
            window = slice(b * rows, b * rows + span + rows)
            mine = slice(b * rows, (b + 1) * rows)
            own = slice(span - b * rows, span + rows)
            for i in range(2):
                query = fqg_ref[i * span + b * rows : i * span + (b + 1) * rows]
                grad = fqg_ref[(2 + i) * span + b * rows : (2 + i) * span + (b + 1) * rows]
                probs, total = softmax(nt(key_s[i, window], query), bias)
                probs_low = probs.astype(BF)
                out_ref[i, :, mine] = nn(value_t[i, :, window], probs_low).astype(BF)
                dscores, delta = score_grads(probs, probs_low, nt(value_s[i, window], grad))
                stats_ref[i * 8 : i * 8 + 1, mine] = total
                stats_ref[i * 8 + 1 : i * 8 + 2, mine] = delta
                dquery_ref[i, mine] = (nn(key_t[i, :, window], dscores) * SCALE).astype(BF).T
                dkey = nn(dscores[own], query) * SCALE
                dvalue = nn(probs_low[own], grad)
                if b == g - 1:
                    dkv_ref[i, 0] = dkey
                    dkv_ref[i, 1] = dvalue
                else:
                    dkv_ref[i, 0, : (b + 1) * rows] += dkey
                    dkv_ref[i, 1, : (b + 1) * rows] += dvalue

    roles(band, lambda: None)


def tail_kernel(g, width_ref, fkv_ref, next_ref, stats_ref, dkv_ref, out_ref):
    line, spot_ = spot(g)
    span = dkv_ref.shape[2]
    rows = span // g

    def band():
        out_ref[...] = dkv_ref[...]

        @pl.when(line < g - 1)
        def _():
            width = width_ref[spot_]
            for b in range(g):
                block = lax.div(lax.broadcasted_iota(jnp.int32, (span - b * rows, rows), 0), BLK)
                bias = jnp.where(block >= WMAX - width, 0.0, -1e30)
                mine = slice(b * rows, (b + 1) * rows)
                for i in range(2):
                    query = next_ref[i * span + b * rows : i * span + (b + 1) * rows]
                    at = (2 + i) * span + b * rows
                    grad = next_ref[at : at + rows]
                    key = fkv_ref[i * span + b * rows : (i + 1) * span]
                    value = fkv_ref[(2 + i) * span + b * rows : (3 + i) * span]
                    total = stats_ref[i * 8 : i * 8 + 1, mine]
                    delta = stats_ref[i * 8 + 1 : i * 8 + 2, mine]
                    probs = jnp.exp2(nt(key, query) * SCALE_2 + bias - total)
                    dscores = (probs * (nt(value, grad) - delta)).astype(BF)
                    out_ref[i, 0, b * rows :] += nn(dscores, query) * SCALE
                    out_ref[i, 1, b * rows :] += nn(probs.astype(BF), grad)

    roles(band, lambda: None)


def copy_kernel(in_ref, out_ref):
    out_ref[...] = in_ref[...]


def weight_kernel(g, out_ref, *refs):
    heads, (og_ref, og_other_ref), near = refs[:g], refs[g : g + 2], refs[g + 2 : -g - 1]
    part_ref, z_refs, sum_s = refs[-g - 1], refs[-g:-1], refs[-1]
    line, spot_ = spot(g)
    rows = og_ref.shape[0]
    chunk = rows // g
    outer = ((og_ref, *near[: g - 1]), (og_other_ref, *near[g - 1 :]))

    def add(part):
        sum_s[...] = sum(part(i, d) for i in range(2) for d in range(g))

    roles(
        lambda: add(lambda i, d: nn(out_ref[i, :, rows_at((spot_ ^ d) * rows, rows)], outer[i][d][...])),
        lambda: add(lambda i, d: tn(heads[d][i * rows : (i + 1) * rows], outer[i][d][...])),
    )
    part_ref[...] = sum_s[rows_at(line * chunk, chunk)]
    for d, ref in enumerate(z_refs, 1):
        ref[...] = sum_s[rows_at((line ^ d) * chunk, chunk)].astype(BF)


def exchange_kernel(dquery_ref, dkv_ref, strided_ref, keep_ref, *rest):
    piece_refs, send_s = rest[:-1], rest[-1]

    def band():
        for i, ref in enumerate((keep_ref, send_s)):
            ref[0] = dquery_ref[i]
            ref[1] = dkv_ref[i, 0].astype(BF)
            ref[2] = dkv_ref[i, 1].astype(BF)

    def strided():
        keep_ref[...] = strided_ref[0]
        send_s[...] = strided_ref[1]

    roles(band, strided)
    size = piece_refs[0].shape[1]
    for n, ref in enumerate(piece_refs):
        ref[...] = send_s[:, n * size : (n + 1) * size]


def sum_kernel(keep_ref, z1_ref, z2_ref, z3_ref, out_ref):
    total = keep_ref[...]
    for ref in (z1_ref, z2_ref, z3_ref):
        total += ref[...].astype(F32)
    out_ref[...] = total.astype(BF)


def gather_kernel(g, pieces, own_ref, g1_ref, g2_ref, g3_ref, keep_ref, *refs):
    line, spot_ = spot(g)
    swapped_refs, out_refs, swapped = refs[:pieces], refs[pieces:-1], refs[-1]
    half_span = swapped_refs[0].shape[1]
    for n, ref in enumerate(swapped_refs):
        swapped[:, n * half_span : (n + 1) * half_span] = ref[...]
    size, width = own_ref.shape
    span = keep_ref.shape[1]
    rows = span // g
    chunk = rows // g
    columns = width // HD
    to_group, to_line = out_refs[:g], out_refs[g:]
    for d, ref in enumerate((own_ref, g1_ref, g2_ref, g3_ref)):
        for n in range(columns):
            for out_ref in to_group:
                out_ref[rows_at(n * g * size + (line ^ d) * size, size)] = ref[:, n * HD : (n + 1) * HD]

    def grads(band, strided):
        for d in range(g):
            for t in range(3):
                at = columns * g * size + t * rows
                to_group[d][at : at + rows] = band[t, rows_at((spot_ ^ d) * rows, rows)]
                for h in range(HS):
                    there = rows_at(h * rows + (line ^ d) * chunk, chunk)
                    to_line[d][(t * HS + h) * chunk : (t * HS + h + 1) * chunk] = strided[t, there]

    roles(lambda: grads(keep_ref, swapped), lambda: grads(swapped, keep_ref))


def finish_kernel(g, *refs):
    from_group, from_line = refs[:g], refs[g : 2 * g]
    outs, weight_ref, grads_s, weight_s, sems = refs[2 * g : 2 * g + 3], *refs[2 * g + 3 :]
    line, spot_ = spot(g)
    rows, width = grads_s.shape[1:]
    half = width // 2
    chunk = rows // g
    size = weight_s.shape[0] // g
    columns = width // HD
    copies = []
    for t in range(3):
        for d in range(g):
            at = columns * size + t * rows
            grads_s[t, :, rows_at((spot_ ^ d) * HD, HD)] = from_group[d][at : at + rows]
            for h in range(HS):
                lanes = slice(half + h * HD, half + (h + 1) * HD)
                at = (t * HS + h) * chunk
                grads_s[t, rows_at((line ^ d) * chunk, chunk), lanes] = from_line[d][at : at + chunk]
        copies.append(pltpu.make_async_copy(grads_s.at[t], outs[t], sems.at[t]))
        copies[-1].start()
    for d in range(g):
        there = rows_at((spot_ ^ d) * size, size)
        for n in range(columns):
            weight_s[there, n * HD : (n + 1) * HD] = from_group[d][n * size : (n + 1) * size]
        copies.append(pltpu.make_async_copy(weight_s.at[there], weight_ref.at[there], sems.at[3 + d]))
        copies[-1].start()
    for copy in copies:
        copy.wait()


def body_roles(g, queries, keys, values, out_grad, out_weight, band_width, col_reach):
    q, k, v, og = queries[0], keys[0], values[0], out_grad[0]
    rows, width = q.shape
    half = width // 2
    span = g * rows
    chunk = rows // g
    devices = lax.axis_size("seq")
    both = ("dp", "seq")

    def send(value, target):
        pairs = []
        for role in range(2):
            for line in range(g):
                for place in range(g):
                    to = target(role, line, place)
                    if to is None:
                        continue
                    to_role, to_line, to_place = to
                    pairs.append((role * devices + line * g + place, to_role * devices + to_line * g + to_place))
        return lax.ppermute(value, both, pairs)

    def swap(value):
        return lax.ppermute(value, "dp", [(0, 1), (1, 0)])

    def by_role(d):
        return lambda role, line, place: (0, line, place ^ d) if role == 0 else (1, line ^ d, place)

    def along_line(d):
        return lambda role, line, place: (role, line ^ d, place)

    def in_group(d):
        return lambda role, line, place: (role, line, place ^ d)

    def shift(step):
        return lambda role, line, place: (0, line + step, place) if role == 0 and 0 <= line + step < g else None

    def ring(step):
        def target(role, line, place):
            to = line + (step if role == 0 else -step)
            return (role, to, place) if 0 <= to < g else (1 - role, line, place)

        return target

    steps = range(1, g)
    role = lax.axis_index("dp")
    og_other = swap(og)
    to_other = jnp.stack([lax.dynamic_slice(value, (0, (1 - role) * half), (rows, half)) for value in (q, k, v)])
    own = jnp.stack([lax.dynamic_slice(value, (0, role * half), (rows, half)) for value in (q, k, v)])
    other = swap(to_other)
    (att,) = call(att_grad_kernel, [shaped((2, rows, half))], [og, og_other, out_weight], name="att_grad")
    packed = call(functools.partial(pack_fields_kernel, g), [shaped((8 * rows, HD))] * (g - 1),
                  [own, other, att], name="pack_fields")
    came = [send(packed[d - 1], by_role(d)) for d in steps]
    near = [send(og, in_group(d)) for d in steps]
    near_other = [swap(value) for value in near]
    fqg, fkv, *back, keep, strided_grads = call(
        functools.partial(forward_kernel, g),
        [shaped((4 * span, HD))] * 2 + [shaped((2 * rows, HD))] * (g - 1)
        + [shaped((2, HS, rows, HD)), shaped((2, 3, span, HD))],
        [col_reach, own, other, att] + came, smem=1, name="forward",
    )
    back = [send(back[d - 1], by_role(d)) for d in steps]
    halo = send(fkv, shift(1))
    *to_heads, mine = call(functools.partial(heads_kernel, g), [shaped((2 * rows, HD))] * g, [keep] + back,
                           name="heads")
    band_out, dquery, dkv, stats = call(
        functools.partial(attention_kernel, g),
        [shaped((2, HD, span)), shaped((2, span, HD)), shaped((2, 2, span, HD), F32), shaped((48, span), F32)],
        [band_width, fqg, fkv, halo], smem=1,
        scratch=[pltpu.VMEM((2, 2 * span, HD), BF), pltpu.VMEM((2, 2 * span, HD), BF),
                 pltpu.VMEM((2, HD, 2 * span), BF), pltpu.VMEM((2, HD, 2 * span), BF)],
        mib=24, name="attention",
    )
    (fqg_copy,) = call(copy_kernel, [shaped(fqg.shape)], [fqg], name="copy")
    following = send(fqg_copy, shift(-1))
    heads = [send(to_heads[d - 1], in_group(d)) for d in steps]
    piece = half // g // g
    parts = call(
        functools.partial(weight_kernel, g), [shaped((piece, width), F32)] + [shaped((piece, width))] * (g - 1),
        [band_out, mine] + heads + [og, og_other] + near + near_other,
        scratch=[pltpu.VMEM((half // g, width), F32)], name="weight",
    )
    summed = [send(parts[d], along_line(d)) for d in steps]
    stats = send(stats, ring(-1))
    (dkv,) = call(functools.partial(tail_kernel, g), [shaped(dkv.shape, F32)],
                  [band_width, fkv, following, stats, dkv], smem=1, order=[summed[-1]], name="tail")
    (piece_sum,) = call(sum_kernel, [shaped((piece, width))], [parts[0]] + summed, order=[dkv], name="sum")
    pieces = [send(piece_sum, along_line(d)) for d in steps]
    grads_kept, *to_other = call(
        exchange_kernel, [shaped((3, span, HD))] + [shaped((3, span // 2, HD))] * 2,
        [dquery, dkv, strided_grads], order=[piece_sum], scratch=[pltpu.VMEM((3, span, HD), BF)], name="exchange",
    )
    packed = call(
        functools.partial(gather_kernel, g, len(to_other)),
        [shaped((half // g * width // HD + 3 * rows, HD))] * g + [shaped((3 * rows, HD))] * g,
        [piece_sum] + pieces + [grads_kept] + [swap(value) for value in to_other],
        scratch=[pltpu.VMEM((3, span, HD), BF)], name="gather_line",
    )
    from_group = [packed[0]] + [send(packed[d], in_group(d)) for d in steps]
    from_line = [packed[g]] + [send(packed[g + d], along_line(d)) for d in steps]
    dq, dk, dv, weight_grad = call(
        functools.partial(finish_kernel, g), [shaped((rows, width))] * 3 + [shaped((half, width))],
        from_group + from_line, left_out=True,
        scratch=[pltpu.VMEM((3, rows, width), BF), pltpu.VMEM((half, width), BF), pltpu.SemaphoreType.DMA((3 + g,))],
        name="finish",
    )
    return dq[None], dk[None], dv[None], weight_grad


def from_behind(value, axis, steps):
    count = lax.axis_size(axis)
    leading, last = (max(0, -steps), min(count, count - steps))
    return lax.ppermute(value, axis, [(source, source + steps) for source in range(leading, last)])


def attend(query_g, key_g, value_g, grad_g, allowed):
    scale = query_g.shape[-1] ** (-0.5)
    scores = jnp.einsum("gqd,gkd->gqk", query_g, key_g, preferred_element_type=F32) * scale
    scores = jnp.where(allowed, scores, -1e30)
    peak = jnp.max(scores, axis=-1, keepdims=True)
    raised = jnp.where(allowed, jnp.exp(scores - peak), 0.0)
    probs = raised / jnp.sum(raised, axis=-1, keepdims=True)
    probs_low = probs.astype(BF)
    output = jnp.einsum("gqk,gkd->gqd", probs_low, value_g, preferred_element_type=F32).astype(BF)
    delta = jnp.sum(grad_g.astype(F32) * output.astype(F32), axis=-1, keepdims=True)
    dprobs = jnp.einsum("gqd,gkd->gqk", grad_g, value_g, preferred_element_type=F32)
    dscores = (probs * (dprobs - delta)).astype(BF)
    d_query = jnp.einsum("gqk,gkd->gqd", dscores, key_g, preferred_element_type=F32) * scale
    d_key = jnp.einsum("gqk,gqd->gkd", dscores, query_g, preferred_element_type=F32) * scale
    d_value = jnp.einsum("gqk,gqd->gkd", probs_low, grad_g, preferred_element_type=F32)
    return (output, d_query, d_key, d_value)


def band_mask(q_pos, k_pos, width):
    lower = (q_pos // BLK)[None, :, None] - width[:, None, None]
    causal = k_pos[None, None, :] <= q_pos[None, :, None]
    inside = k_pos[None, None, :] >= 0
    return causal & inside & ((k_pos // BLK)[None, None, :] >= lower)


def column_mask(count, reach):
    row_q = jnp.arange(count, dtype=jnp.int32)[None, :, None]
    row_k = jnp.arange(count, dtype=jnp.int32)[None, None, :]
    return (row_k <= row_q) & (row_q - row_k < reach[:, None, None])


def column_local(field, reach, devices):
    per_dev = IMW // devices
    count = field.shape[1] // per_dev
    grid = (
        field.reshape(4, count, per_dev, HS, HD)
        .transpose(0, 2, 3, 1, 4)
        .reshape(4, per_dev * HS, count, HD)
    )
    allowed = jnp.tile(column_mask(count, reach), (per_dev, 1, 1))
    output, d_query, d_key, d_value = attend(grid[0], grid[1], grid[2], grid[3], allowed)
    stacked = jnp.stack([output, d_query.astype(BF), d_key.astype(BF), d_value.astype(BF)])
    stacked = stacked.reshape(4, per_dev, HS, count, HD).transpose(0, 3, 1, 2, 4)
    return stacked.reshape(4, count * per_dev, 1, HS, HD)


def heads_first(field, count):
    return field.reshape(count, HB, HD).transpose(1, 0, 2)


def rows_first(field, count):
    return field.transpose(1, 0, 2).reshape(count, HB * HD)


def body_any(queries, keys, values, out_grad, out_weight, band_width, col_reach):
    query_all = queries[0]
    key_all = keys[0]
    value_all = values[0]
    grad_out = out_grad[0]
    rows = query_all.shape[0]
    devices = lax.axis_size("seq")
    place = lax.axis_index("seq")
    band_dim = HB * HD
    att_grad = jnp.einsum(
        "to,ao->ta",
        grad_out,
        lax.all_gather(out_weight, "dp", axis=0, tiled=True),
        preferred_element_type=F32,
    ).astype(BF)
    strided = jnp.stack([field[:, band_dim:] for field in (query_all, key_all, value_all, att_grad)])
    strided = strided.reshape(4, rows // devices, devices, HS, HD)
    column_major = lax.all_to_all(strided, "seq", split_axis=2, concat_axis=1, tiled=True)
    column_result = column_local(column_major, col_reach, devices)
    row_major = lax.all_to_all(
        column_result, "seq", split_axis=1, concat_axis=2, tiled=True
    ).reshape(4, rows, HS * HD)
    kv_own = (key_all[:, :band_dim], value_all[:, :band_dim])
    reach_dev = -(-(WMAX * BLK) // rows)
    earlier = []
    for hop in range(reach_dev, 0, -1):
        earlier.append(from_behind((kv_own[0], kv_own[1]), "seq", hop))
    key_window = jnp.concatenate([pair[0] for pair in earlier] + [kv_own[0]], 0)
    value_window = jnp.concatenate([pair[1] for pair in earlier] + [kv_own[1]], 0)
    width_all = (reach_dev + 1) * rows
    q_pos = place * rows + jnp.arange(rows, dtype=jnp.int32)
    k_pos = (place - reach_dev) * rows + jnp.arange(width_all, dtype=jnp.int32)
    allowed = band_mask(q_pos, k_pos, band_width)
    band_out, band_dq, band_dk, band_dv = attend(
        heads_first(query_all[:, :band_dim], rows),
        heads_first(key_window, width_all),
        heads_first(value_window, width_all),
        heads_first(att_grad[:, :band_dim], rows),
        allowed,
    )
    key_rows = rows_first(band_dk, width_all)
    value_rows = rows_first(band_dv, width_all)
    key_total = key_rows[reach_dev * rows :]
    value_total = value_rows[reach_dev * rows :]
    for hop in range(1, reach_dev + 1):
        slot = (reach_dev - hop) * rows
        key_total += from_behind(key_rows[slot : slot + rows].astype(BF), "seq", -hop).astype(F32)
        value_total += from_behind(value_rows[slot : slot + rows].astype(BF), "seq", -hop).astype(F32)
    attn_out = jnp.concatenate([rows_first(band_out, rows), row_major[0]], 1)
    query_grad = jnp.concatenate([rows_first(band_dq, rows).astype(BF), row_major[1]], 1)
    key_grad = jnp.concatenate([key_total.astype(BF), row_major[2]], 1)
    value_grad = jnp.concatenate([value_total.astype(BF), row_major[3]], 1)
    shared = lax.psum_scatter(
        jnp.einsum("ta,to->ao", attn_out, grad_out, preferred_element_type=F32).astype(BF),
        "dp",
        scatter_dimension=0,
        tiled=True,
    ).astype(F32)
    weight_grad = lax.psum(shared, "seq")
    return (query_grad[None], key_grad[None], value_grad[None], weight_grad.astype(BF))


def solution(mesh):
    def body(*args):
        rows = args[0].shape[1]
        devices = mesh.shape["seq"]
        g = IMW // rows
        fits = (
            mesh.shape["dp"] == 2
            and rows == BLK
            and devices == g * g
            and g == HB == HS == 4
            and WMAX * BLK == IMW
            and args[4].shape[0] == HB * HD == HS * HD
        )
        return body_roles(g, *args) if fits else body_any(*args)

    return jax.shard_map(
        body,
        mesh=mesh,
        in_specs=(
            P("dp", "seq", None),
            P("dp", "seq", None),
            P("dp", "seq", None),
            P("dp", "seq", None),
            P("dp", None),
            P(),
            P(),
        ),
        out_specs=(P("dp", "seq", None), P("dp", "seq", None), P("dp", "seq", None), P("dp", None)),
        check_vma=False,
    )
```

```python
import functools
import math

import jax
import jax.numpy as jnp
from jax import lax
from jax.experimental import pallas as pl
from jax.experimental.pallas import tpu as pltpu
from jax.sharding import PartitionSpec as P

HD = 128
HB = 4
HS = 4
IMW = 512
BLK = 128
WMAX = 4

BF = jnp.bfloat16
F32 = jnp.float32
MIB = 1 << 20


def nn(a, b):
    return lax.dot_general(a, b, (((1,), (0,)), ((), ())), preferred_element_type=F32)


def nt(a, b):
    return lax.dot_general(a, b, (((1,), (1,)), ((), ())), preferred_element_type=F32)


def tn(a, b):
    return lax.dot_general(a, b, (((0,), (0,)), ((), ())), preferred_element_type=F32)


def rows_at(start, size):
    return pl.ds(pl.multiple_of(start, size), size)


def shaped(shape, dtype=BF):
    return jax.ShapeDtypeStruct(shape, dtype)


def call(kernel, outs, args, smem=0, left_out=False, order=(), scratch=(), mib=16, name=None):
    vmem = pl.BlockSpec(memory_space=pltpu.VMEM)
    scalars = pl.BlockSpec(memory_space=pltpu.SMEM)
    anywhere = pl.BlockSpec(memory_space=pl.ANY)
    count = len(args)

    def body(*refs):
        kernel(*refs[:count], *refs[count + len(order) :])

    return pl.pallas_call(
        body,
        out_shape=outs,
        in_specs=[scalars] * smem + [vmem] * (count - smem) + [anywhere] * len(order),
        out_specs=[anywhere if left_out else vmem] * len(outs),
        scratch_shapes=list(scratch),
        compiler_params=pltpu.CompilerParams(vmem_limit_bytes=mib * MIB),
        name=name,
    )(*args, *order)


def roles(band, strided):
    role = lax.axis_index("dp")
    pl.when(role == 0)(band)
    pl.when(role == 1)(strided)


def spot(g):
    place = lax.axis_index("seq")
    return lax.div(place, g), lax.rem(place, g)


def read_field(own_ref, other_ref, att_ref, i, t):
    if t == 3:
        return lambda rows, lanes: att_ref[i, rows, lanes]
    return lambda rows, lanes: (own_ref, other_ref)[i][t, rows, lanes]


def pack_fields_kernel(g, own_ref, other_ref, att_ref, *out_refs):
    line, spot_ = spot(g)
    rows = own_ref.shape[1]
    chunk = rows // g
    fields = [(i, t, read_field(own_ref, other_ref, att_ref, i, t)) for i in range(2) for t in range(4)]

    def band():
        for d in range(1, g):
            for i, t, read in fields:
                at = (i * 4 + t) * rows
                out_refs[d - 1][at : at + rows] = read(slice(None), rows_at((spot_ ^ d) * HD, HD))

    def strided():
        for d in range(1, g):
            there = rows_at((line ^ d) * chunk, chunk)
            for i, t, read in fields:
                for h in range(HS):
                    at = (i * 4 + t) * rows + h * chunk
                    out_refs[d - 1][at : at + chunk] = read(there, slice(h * HD, (h + 1) * HD))

    roles(band, strided)


def att_grad_kernel(own_ref, other_ref, weight_ref, out_ref):
    out_ref[0] = nt(own_ref[...], weight_ref[...]).astype(BF)
    out_ref[1] = nt(other_ref[...], weight_ref[...]).astype(BF)


def strided_bias(rows, chunk, reach):
    key = lax.broadcasted_iota(jnp.int32, (rows, rows), 0)
    query = lax.broadcasted_iota(jnp.int32, (rows, rows), 1)
    apart = lax.div(query, chunk) - lax.div(key, chunk)
    same = lax.rem(key, chunk) == lax.rem(query, chunk)
    return jnp.where(same & (apart >= 0) & (apart < reach), 0.0, -1e30)


def score_grads(probs, probs_low, dprobs):
    delta = jnp.sum(probs_low.astype(F32) * dprobs, axis=0, keepdims=True)
    return (probs * (dprobs - delta)).astype(BF), delta


SCALE = HD ** (-0.5)
SCALE_2 = SCALE / math.log(2)


def softmax(scores, bias):
    scores = scores * SCALE_2 + bias
    peak = jnp.max(scores, axis=0, keepdims=True)
    raised = jnp.exp2(scores - peak)
    total = jnp.sum(raised, axis=0, keepdims=True)
    return raised * (1.0 / total), peak + jnp.log2(total)


def forward_kernel(g, reach_ref, own_ref, other_ref, att_ref, r1_ref, r2_ref, r3_ref,
                   fqg_ref, fkv_ref, o1_ref, o2_ref, o3_ref, keep_ref, grads_ref):
    line, spot_ = spot(g)
    rows = own_ref.shape[1]
    span = g * rows
    chunk = rows // g
    came = (r1_ref, r2_ref, r3_ref)
    back = (o1_ref, o2_ref, o3_ref)
    fields = [(i, t, read_field(own_ref, other_ref, att_ref, i, t)) for i in range(2) for t in range(4)]

    def put(i, t, start, size, value):
        ref = (fqg_ref, fkv_ref, fkv_ref, fqg_ref)[t]
        ref[rows_at((t // 2 * 2 + i) * span + start, size)] = value

    def band():
        for i, t, read in fields:
            at = (i * 4 + t) * rows
            put(i, t, spot_ * rows, rows, read(slice(None), rows_at(spot_ * HD, HD)))
            for d in range(1, g):
                put(i, t, (spot_ ^ d) * rows, rows, came[d - 1][at : at + rows])

    def strided():
        here = rows_at(line * chunk, chunk)
        for i, t, read in fields:
            for h in range(HS):
                at = (i * 4 + t) * rows + h * chunk
                put(i, t, h * rows + line * chunk, chunk, read(here, slice(h * HD, (h + 1) * HD)))
                for d in range(1, g):
                    put(i, t, h * rows + (line ^ d) * chunk, chunk, came[d - 1][at : at + chunk])
        each = [(i, h) for h in range(HS) for i in range(2)]

        def head(t, i, h):
            at = (t // 2 * 2 + i) * span + h * rows
            return (fqg_ref, fkv_ref, fkv_ref, fqg_ref)[t][at : at + rows]

        scores, dprobs, probs = {}, {}, {}
        for i, h in each:
            scores[i, h] = nt(head(1, i, h), head(0, i, h))
            dprobs[i, h] = nt(head(2, i, h), head(3, i, h))
        for h in range(HS):
            bias = strided_bias(rows, chunk, reach_ref[h])
            for i in range(2):
                probs[i, h], _ = softmax(scores[i, h], bias)
        for i, h in each:
            keep_ref[i, h] = tn(probs[i, h].astype(BF), head(2, i, h)).astype(BF)
        for d in range(1, g):
            there = rows_at((line ^ d) * chunk, chunk)
            for i, h in each:
                at = (i * HS + h) * chunk
                back[d - 1][at : at + chunk] = keep_ref[i, h, there]
        for i, h in each:
            mine = slice(h * rows, (h + 1) * rows)
            probs_low = probs[i, h].astype(BF)
            dscores, _ = score_grads(probs[i, h], probs_low, dprobs[i, h])
            grads_ref[i, 0, mine] = (tn(dscores, head(1, i, h)) * SCALE).astype(BF)
            grads_ref[i, 1, mine] = (nn(dscores, head(0, i, h)) * SCALE).astype(BF)
            grads_ref[i, 2, mine] = nn(probs_low, head(3, i, h)).astype(BF)

    roles(band, strided)


def heads_kernel(g, keep_ref, o1_ref, o2_ref, o3_ref, p1_ref, p2_ref, p3_ref, mine_ref):
    line, spot_ = spot(g)
    rows = keep_ref.shape[2]
    chunk = rows // g
    came = (o1_ref, o2_ref, o3_ref)
    outs = (mine_ref, p1_ref, p2_ref, p3_ref)

    def strided():
        for to in range(g):
            head = spot_ ^ to
            for i in range(2):
                outs[to][rows_at(i * rows + line * chunk, chunk)] = keep_ref[i, head, rows_at(line * chunk, chunk)]
                for d in range(1, g):
                    source = rows_at((i * HS + head) * chunk, chunk)
                    outs[to][rows_at(i * rows + (line ^ d) * chunk, chunk)] = came[d - 1][source]

    roles(lambda: None, strided)


def attention_kernel(g, width_ref, fqg_ref, fkv_ref, halo_ref,
                     out_ref, dquery_ref, dkv_ref, stats_ref, key_s, value_s, key_t, value_t):
    line, spot_ = spot(g)
    span = dquery_ref.shape[1]
    rows = span // g

    def band():
        width = width_ref[spot_]
        key_at = lax.broadcasted_iota(jnp.int32, (span + rows, rows), 0)
        query_at = lax.broadcasted_iota(jnp.int32, (span + rows, rows), 1)
        block = lax.div(key_at, BLK)
        near = (block >= WMAX - width) & (key_at - span <= query_at)
        for i in range(2):
            for t, ref in enumerate((key_s, value_s)):
                at = (t * 2 + i) * span
                ref[i, span:] = fkv_ref[at : at + span]
                ref[i, :span] = halo_ref[at : at + span]
            key_t[i] = key_s[i].T
            value_t[i] = value_s[i].T
        for b in reversed(range(g)):
            bias = jnp.where(near & ((block + b >= g) | (line > 0)), 0.0, -1e30)
            window = slice(b * rows, b * rows + span + rows)
            mine = slice(b * rows, (b + 1) * rows)
            own = slice(span - b * rows, span + rows)
            both = range(2)
            query = [fqg_ref[i * span + b * rows : i * span + (b + 1) * rows] for i in both]
            grad = [fqg_ref[(2 + i) * span + b * rows : (2 + i) * span + (b + 1) * rows] for i in both]
            scores = [nt(key_s[i, window], query[i]) for i in both]
            dprobs = [nt(value_s[i, window], grad[i]) for i in both]
            probs, total = zip(*[softmax(scores[i], bias) for i in both])
            probs_low = [probs[i].astype(BF) for i in both]
            outputs = [nn(value_t[i, :, window], probs_low[i]) for i in both]
            dvalue = [nn(probs_low[i][own], grad[i]) for i in both]
            dscores, delta = zip(*[score_grads(probs[i], probs_low[i], dprobs[i]) for i in both])
            dquery = [nn(key_t[i, :, window], dscores[i]) for i in both]
            dkey = [nn(dscores[i][own], query[i]) * SCALE for i in both]
            for i in both:
                out_ref[i, :, mine] = outputs[i].astype(BF)
                stats_ref[i * 8 : i * 8 + 1, mine] = total[i]
                stats_ref[i * 8 + 1 : i * 8 + 2, mine] = delta[i]
                dquery_ref[i, mine] = (dquery[i] * SCALE).astype(BF).T
                if b == g - 1:
                    dkv_ref[i, 0] = dkey[i]
                    dkv_ref[i, 1] = dvalue[i]
                else:
                    dkv_ref[i, 0, : (b + 1) * rows] += dkey[i]
                    dkv_ref[i, 1, : (b + 1) * rows] += dvalue[i]

    roles(band, lambda: None)


def tail_kernel(g, width_ref, fkv_ref, next_ref, stats_ref, dkv_ref, out_ref):
    line, spot_ = spot(g)
    span = dkv_ref.shape[2]
    rows = span // g

    def band():
        out_ref[...] = dkv_ref[...]

        @pl.when(line < g - 1)
        def _():
            width = width_ref[spot_]
            for b in range(g):
                block = lax.div(lax.broadcasted_iota(jnp.int32, (span - b * rows, rows), 0), BLK)
                bias = jnp.where(block >= WMAX - width, 0.0, -1e30)
                mine = slice(b * rows, (b + 1) * rows)
                both = range(2)
                query = [next_ref[i * span + b * rows : i * span + (b + 1) * rows] for i in both]
                grad = [next_ref[(2 + i) * span + b * rows : (2 + i) * span + (b + 1) * rows] for i in both]
                scores = [nt(fkv_ref[i * span + b * rows : (i + 1) * span], query[i]) for i in both]
                dprobs = [nt(fkv_ref[(2 + i) * span + b * rows : (3 + i) * span], grad[i]) for i in both]
                probs = [
                    jnp.exp2(scores[i] * SCALE_2 + bias - stats_ref[i * 8 : i * 8 + 1, mine]) for i in both
                ]
                dvalue = [nn(probs[i].astype(BF), grad[i]) for i in both]
                dscores = [
                    (probs[i] * (dprobs[i] - stats_ref[i * 8 + 1 : i * 8 + 2, mine])).astype(BF) for i in both
                ]
                dkey = [nn(dscores[i], query[i]) * SCALE for i in both]
                for i in both:
                    out_ref[i, 0, b * rows :] += dkey[i]
                    out_ref[i, 1, b * rows :] += dvalue[i]

    roles(band, lambda: None)


def copy_kernel(in_ref, out_ref):
    out_ref[...] = in_ref[...]


def weight_kernel(g, out_ref, *refs):
    heads, (og_ref, og_other_ref), near = refs[:g], refs[g : g + 2], refs[g + 2 : -g - 1]
    part_ref, z_refs, sum_s = refs[-g - 1], refs[-g:-1], refs[-1]
    line, spot_ = spot(g)
    rows = og_ref.shape[0]
    chunk = rows // g
    outer = ((og_ref, *near[: g - 1]), (og_other_ref, *near[g - 1 :]))

    def add(part):
        sum_s[...] = sum(part(i, d) for i in range(2) for d in range(g))

    roles(
        lambda: add(lambda i, d: nn(out_ref[i, :, rows_at((spot_ ^ d) * rows, rows)], outer[i][d][...])),
        lambda: add(lambda i, d: tn(heads[d][i * rows : (i + 1) * rows], outer[i][d][...])),
    )
    part_ref[...] = sum_s[rows_at(line * chunk, chunk)]
    for d, ref in enumerate(z_refs, 1):
        ref[...] = sum_s[rows_at((line ^ d) * chunk, chunk)].astype(BF)


def exchange_kernel(dquery_ref, dkv_ref, strided_ref, keep_ref, *rest):
    piece_refs, send_s = rest[:-1], rest[-1]

    def band():
        for i, ref in enumerate((keep_ref, send_s)):
            ref[0] = dquery_ref[i]
            ref[1] = dkv_ref[i, 0].astype(BF)
            ref[2] = dkv_ref[i, 1].astype(BF)

    def strided():
        keep_ref[...] = strided_ref[0]
        send_s[...] = strided_ref[1]

    roles(band, strided)
    size = piece_refs[0].shape[1]
    for n, ref in enumerate(piece_refs):
        ref[...] = send_s[:, n * size : (n + 1) * size]


def sum_kernel(keep_ref, z1_ref, z2_ref, z3_ref, out_ref):
    total = keep_ref[...]
    for ref in (z1_ref, z2_ref, z3_ref):
        total += ref[...].astype(F32)
    out_ref[...] = total.astype(BF)


def gather_kernel(g, pieces, own_ref, g1_ref, g2_ref, g3_ref, keep_ref, *refs):
    line, spot_ = spot(g)
    swapped_refs, out_refs, swapped = refs[:pieces], refs[pieces:-1], refs[-1]
    half_span = swapped_refs[0].shape[1]
    for n, ref in enumerate(swapped_refs):
        swapped[:, n * half_span : (n + 1) * half_span] = ref[...]
    size, width = own_ref.shape
    span = keep_ref.shape[1]
    rows = span // g
    chunk = rows // g
    columns = width // HD
    to_group, to_line = out_refs[:g], out_refs[g:]
    for d, ref in enumerate((own_ref, g1_ref, g2_ref, g3_ref)):
        for n in range(columns):
            for out_ref in to_group:
                out_ref[rows_at(n * g * size + (line ^ d) * size, size)] = ref[:, n * HD : (n + 1) * HD]

    def grads(band, strided):
        for d in range(g):
            for t in range(3):
                at = columns * g * size + t * rows
                to_group[d][at : at + rows] = band[t, rows_at((spot_ ^ d) * rows, rows)]
                for h in range(HS):
                    there = rows_at(h * rows + (line ^ d) * chunk, chunk)
                    to_line[d][(t * HS + h) * chunk : (t * HS + h + 1) * chunk] = strided[t, there]

    roles(lambda: grads(keep_ref, swapped), lambda: grads(swapped, keep_ref))


def finish_kernel(g, *refs):
    from_group, from_line = refs[:g], refs[g : 2 * g]
    outs, weight_ref, grads_s, weight_s, sems = refs[2 * g : 2 * g + 3], *refs[2 * g + 3 :]
    line, spot_ = spot(g)
    rows, width = grads_s.shape[1:]
    half = width // 2
    chunk = rows // g
    size = weight_s.shape[0] // g
    columns = width // HD
    copies = []
    for t in range(3):
        for d in range(g):
            at = columns * size + t * rows
            grads_s[t, :, rows_at((spot_ ^ d) * HD, HD)] = from_group[d][at : at + rows]
            for h in range(HS):
                lanes = slice(half + h * HD, half + (h + 1) * HD)
                at = (t * HS + h) * chunk
                grads_s[t, rows_at((line ^ d) * chunk, chunk), lanes] = from_line[d][at : at + chunk]
        copies.append(pltpu.make_async_copy(grads_s.at[t], outs[t], sems.at[t]))
        copies[-1].start()
    for d in range(g):
        there = rows_at((spot_ ^ d) * size, size)
        for n in range(columns):
            weight_s[there, n * HD : (n + 1) * HD] = from_group[d][n * size : (n + 1) * size]
        copies.append(pltpu.make_async_copy(weight_s.at[there], weight_ref.at[there], sems.at[3 + d]))
        copies[-1].start()
    for copy in copies:
        copy.wait()


def body_roles(g, queries, keys, values, out_grad, out_weight, band_width, col_reach):
    q, k, v, og = queries[0], keys[0], values[0], out_grad[0]
    rows, width = q.shape
    half = width // 2
    span = g * rows
    chunk = rows // g
    devices = lax.axis_size("seq")
    both = ("dp", "seq")

    def send(value, target):
        pairs = []
        for role in range(2):
            for line in range(g):
                for place in range(g):
                    to = target(role, line, place)
                    if to is None:
                        continue
                    to_role, to_line, to_place = to
                    pairs.append((role * devices + line * g + place, to_role * devices + to_line * g + to_place))
        return lax.ppermute(value, both, pairs)

    def swap(value):
        return lax.ppermute(value, "dp", [(0, 1), (1, 0)])

    def by_role(d):
        return lambda role, line, place: (0, line, place ^ d) if role == 0 else (1, line ^ d, place)

    def along_line(d):
        return lambda role, line, place: (role, line ^ d, place)

    def in_group(d):
        return lambda role, line, place: (role, line, place ^ d)

    def shift(step):
        return lambda role, line, place: (0, line + step, place) if role == 0 and 0 <= line + step < g else None

    def ring(step):
        def target(role, line, place):
            to = line + (step if role == 0 else -step)
            return (role, to, place) if 0 <= to < g else (1 - role, line, place)

        return target

    steps = range(1, g)
    role = lax.axis_index("dp")
    og_other = swap(og)
    to_other = jnp.stack([lax.dynamic_slice(value, (0, (1 - role) * half), (rows, half)) for value in (q, k, v)])
    own = jnp.stack([lax.dynamic_slice(value, (0, role * half), (rows, half)) for value in (q, k, v)])
    other = swap(to_other)
    (att,) = call(att_grad_kernel, [shaped((2, rows, half))], [og, og_other, out_weight], name="att_grad")
    packed = call(functools.partial(pack_fields_kernel, g), [shaped((8 * rows, HD))] * (g - 1),
                  [own, other, att], name="pack_fields")
    came = [send(packed[d - 1], by_role(d)) for d in steps]
    near = [send(og, in_group(d)) for d in steps]
    near_other = [swap(value) for value in near]
    fqg, fkv, *back, keep, strided_grads = call(
        functools.partial(forward_kernel, g),
        [shaped((4 * span, HD))] * 2 + [shaped((2 * rows, HD))] * (g - 1)
        + [shaped((2, HS, rows, HD)), shaped((2, 3, span, HD))],
        [col_reach, own, other, att] + came, smem=1, name="forward",
    )
    back = [send(back[d - 1], by_role(d)) for d in steps]
    halo = send(fkv, shift(1))
    *to_heads, mine = call(functools.partial(heads_kernel, g), [shaped((2 * rows, HD))] * g, [keep] + back,
                           name="heads")
    band_out, dquery, dkv, stats = call(
        functools.partial(attention_kernel, g),
        [shaped((2, HD, span)), shaped((2, span, HD)), shaped((2, 2, span, HD), F32), shaped((48, span), F32)],
        [band_width, fqg, fkv, halo], smem=1,
        scratch=[pltpu.VMEM((2, 2 * span, HD), BF), pltpu.VMEM((2, 2 * span, HD), BF),
                 pltpu.VMEM((2, HD, 2 * span), BF), pltpu.VMEM((2, HD, 2 * span), BF)],
        mib=24, name="attention",
    )
    (fqg_copy,) = call(copy_kernel, [shaped(fqg.shape)], [fqg], name="copy")
    following = send(fqg_copy, shift(-1))
    heads = [send(to_heads[d - 1], in_group(d)) for d in steps]
    piece = half // g // g
    parts = call(
        functools.partial(weight_kernel, g), [shaped((piece, width), F32)] + [shaped((piece, width))] * (g - 1),
        [band_out, mine] + heads + [og, og_other] + near + near_other,
        scratch=[pltpu.VMEM((half // g, width), F32)], name="weight",
    )
    summed = [send(parts[d], along_line(d)) for d in steps]
    stats = send(stats, ring(-1))
    (dkv,) = call(functools.partial(tail_kernel, g), [shaped(dkv.shape, F32)],
                  [band_width, fkv, following, stats, dkv], smem=1, order=[summed[-1]], name="tail")
    (piece_sum,) = call(sum_kernel, [shaped((piece, width))], [parts[0]] + summed, order=[dkv], name="sum")
    pieces = [send(piece_sum, along_line(d)) for d in steps]
    grads_kept, *to_other = call(
        exchange_kernel, [shaped((3, span, HD))] + [shaped((3, span // 2, HD))] * 2,
        [dquery, dkv, strided_grads], order=[piece_sum], scratch=[pltpu.VMEM((3, span, HD), BF)], name="exchange",
    )
    packed = call(
        functools.partial(gather_kernel, g, len(to_other)),
        [shaped((half // g * width // HD + 3 * rows, HD))] * g + [shaped((3 * rows, HD))] * g,
        [piece_sum] + pieces + [grads_kept] + [swap(value) for value in to_other],
        scratch=[pltpu.VMEM((3, span, HD), BF)], name="gather_line",
    )
    from_group = [packed[0]] + [send(packed[d], in_group(d)) for d in steps]
    from_line = [packed[g]] + [send(packed[g + d], along_line(d)) for d in steps]
    dq, dk, dv, weight_grad = call(
        functools.partial(finish_kernel, g), [shaped((rows, width))] * 3 + [shaped((half, width))],
        from_group + from_line, left_out=True,
        scratch=[pltpu.VMEM((3, rows, width), BF), pltpu.VMEM((half, width), BF), pltpu.SemaphoreType.DMA((3 + g,))],
        name="finish",
    )
    return dq[None], dk[None], dv[None], weight_grad


def from_behind(value, axis, steps):
    count = lax.axis_size(axis)
    leading, last = (max(0, -steps), min(count, count - steps))
    return lax.ppermute(value, axis, [(source, source + steps) for source in range(leading, last)])


def attend(query_g, key_g, value_g, grad_g, allowed):
    scale = query_g.shape[-1] ** (-0.5)
    scores = jnp.einsum("gqd,gkd->gqk", query_g, key_g, preferred_element_type=F32) * scale
    scores = jnp.where(allowed, scores, -1e30)
    peak = jnp.max(scores, axis=-1, keepdims=True)
    raised = jnp.where(allowed, jnp.exp(scores - peak), 0.0)
    probs = raised / jnp.sum(raised, axis=-1, keepdims=True)
    probs_low = probs.astype(BF)
    output = jnp.einsum("gqk,gkd->gqd", probs_low, value_g, preferred_element_type=F32).astype(BF)
    delta = jnp.sum(grad_g.astype(F32) * output.astype(F32), axis=-1, keepdims=True)
    dprobs = jnp.einsum("gqd,gkd->gqk", grad_g, value_g, preferred_element_type=F32)
    dscores = (probs * (dprobs - delta)).astype(BF)
    d_query = jnp.einsum("gqk,gkd->gqd", dscores, key_g, preferred_element_type=F32) * scale
    d_key = jnp.einsum("gqk,gqd->gkd", dscores, query_g, preferred_element_type=F32) * scale
    d_value = jnp.einsum("gqk,gqd->gkd", probs_low, grad_g, preferred_element_type=F32)
    return (output, d_query, d_key, d_value)


def band_mask(q_pos, k_pos, width):
    lower = (q_pos // BLK)[None, :, None] - width[:, None, None]
    causal = k_pos[None, None, :] <= q_pos[None, :, None]
    inside = k_pos[None, None, :] >= 0
    return causal & inside & ((k_pos // BLK)[None, None, :] >= lower)


def column_mask(count, reach):
    row_q = jnp.arange(count, dtype=jnp.int32)[None, :, None]
    row_k = jnp.arange(count, dtype=jnp.int32)[None, None, :]
    return (row_k <= row_q) & (row_q - row_k < reach[:, None, None])


def column_local(field, reach, devices):
    per_dev = IMW // devices
    count = field.shape[1] // per_dev
    grid = (
        field.reshape(4, count, per_dev, HS, HD)
        .transpose(0, 2, 3, 1, 4)
        .reshape(4, per_dev * HS, count, HD)
    )
    allowed = jnp.tile(column_mask(count, reach), (per_dev, 1, 1))
    output, d_query, d_key, d_value = attend(grid[0], grid[1], grid[2], grid[3], allowed)
    stacked = jnp.stack([output, d_query.astype(BF), d_key.astype(BF), d_value.astype(BF)])
    stacked = stacked.reshape(4, per_dev, HS, count, HD).transpose(0, 3, 1, 2, 4)
    return stacked.reshape(4, count * per_dev, 1, HS, HD)


def heads_first(field, count):
    return field.reshape(count, HB, HD).transpose(1, 0, 2)


def rows_first(field, count):
    return field.transpose(1, 0, 2).reshape(count, HB * HD)


def body_any(queries, keys, values, out_grad, out_weight, band_width, col_reach):
    query_all = queries[0]
    key_all = keys[0]
    value_all = values[0]
    grad_out = out_grad[0]
    rows = query_all.shape[0]
    devices = lax.axis_size("seq")
    place = lax.axis_index("seq")
    band_dim = HB * HD
    att_grad = jnp.einsum(
        "to,ao->ta",
        grad_out,
        lax.all_gather(out_weight, "dp", axis=0, tiled=True),
        preferred_element_type=F32,
    ).astype(BF)
    strided = jnp.stack([field[:, band_dim:] for field in (query_all, key_all, value_all, att_grad)])
    strided = strided.reshape(4, rows // devices, devices, HS, HD)
    column_major = lax.all_to_all(strided, "seq", split_axis=2, concat_axis=1, tiled=True)
    column_result = column_local(column_major, col_reach, devices)
    row_major = lax.all_to_all(
        column_result, "seq", split_axis=1, concat_axis=2, tiled=True
    ).reshape(4, rows, HS * HD)
    kv_own = (key_all[:, :band_dim], value_all[:, :band_dim])
    reach_dev = -(-(WMAX * BLK) // rows)
    earlier = []
    for hop in range(reach_dev, 0, -1):
        earlier.append(from_behind((kv_own[0], kv_own[1]), "seq", hop))
    key_window = jnp.concatenate([pair[0] for pair in earlier] + [kv_own[0]], 0)
    value_window = jnp.concatenate([pair[1] for pair in earlier] + [kv_own[1]], 0)
    width_all = (reach_dev + 1) * rows
    q_pos = place * rows + jnp.arange(rows, dtype=jnp.int32)
    k_pos = (place - reach_dev) * rows + jnp.arange(width_all, dtype=jnp.int32)
    allowed = band_mask(q_pos, k_pos, band_width)
    band_out, band_dq, band_dk, band_dv = attend(
        heads_first(query_all[:, :band_dim], rows),
        heads_first(key_window, width_all),
        heads_first(value_window, width_all),
        heads_first(att_grad[:, :band_dim], rows),
        allowed,
    )
    key_rows = rows_first(band_dk, width_all)
    value_rows = rows_first(band_dv, width_all)
    key_total = key_rows[reach_dev * rows :]
    value_total = value_rows[reach_dev * rows :]
    for hop in range(1, reach_dev + 1):
        slot = (reach_dev - hop) * rows
        key_total += from_behind(key_rows[slot : slot + rows].astype(BF), "seq", -hop).astype(F32)
        value_total += from_behind(value_rows[slot : slot + rows].astype(BF), "seq", -hop).astype(F32)
    attn_out = jnp.concatenate([rows_first(band_out, rows), row_major[0]], 1)
    query_grad = jnp.concatenate([rows_first(band_dq, rows).astype(BF), row_major[1]], 1)
    key_grad = jnp.concatenate([key_total.astype(BF), row_major[2]], 1)
    value_grad = jnp.concatenate([value_total.astype(BF), row_major[3]], 1)
    shared = lax.psum_scatter(
        jnp.einsum("ta,to->ao", attn_out, grad_out, preferred_element_type=F32).astype(BF),
        "dp",
        scatter_dimension=0,
        tiled=True,
    ).astype(F32)
    weight_grad = lax.psum(shared, "seq")
    return (query_grad[None], key_grad[None], value_grad[None], weight_grad.astype(BF))


def solution(mesh):
    def body(*args):
        rows = args[0].shape[1]
        devices = mesh.shape["seq"]
        g = IMW // rows
        fits = (
            mesh.shape["dp"] == 2
            and rows == BLK
            and devices == g * g
            and g == HB == HS == 4
            and WMAX * BLK == IMW
            and args[4].shape[0] == HB * HD == HS * HD
        )
        return body_roles(g, *args) if fits else body_any(*args)

    return jax.shard_map(
        body,
        mesh=mesh,
        in_specs=(
            P("dp", "seq", None),
            P("dp", "seq", None),
            P("dp", "seq", None),
            P("dp", "seq", None),
            P("dp", None),
            P(),
            P(),
        ),
        out_specs=(P("dp", "seq", None), P("dp", "seq", None), P("dp", "seq", None), P("dp", None)),
        check_vma=False,
    )
```

```python
import functools
import math

import jax
import jax.numpy as jnp
from jax import lax
from jax.experimental import pallas as pl
from jax.experimental.pallas import tpu as pltpu
from jax.sharding import PartitionSpec as P

HD = 128
HB = 4
HS = 4
IMW = 512
BLK = 128
WMAX = 4

BF = jnp.bfloat16
F32 = jnp.float32
MIB = 1 << 20


def nn(a, b):
    return lax.dot_general(a, b, (((1,), (0,)), ((), ())), preferred_element_type=F32)


def nt(a, b):
    return lax.dot_general(a, b, (((1,), (1,)), ((), ())), preferred_element_type=F32)


def tn(a, b):
    return lax.dot_general(a, b, (((0,), (0,)), ((), ())), preferred_element_type=F32)


def rows_at(start, size):
    return pl.ds(pl.multiple_of(start, size), size)


def shaped(shape, dtype=BF):
    return jax.ShapeDtypeStruct(shape, dtype)


def call(kernel, outs, args, smem=0, left_out=False, order=(), scratch=(), mib=16, name=None):
    vmem = pl.BlockSpec(memory_space=pltpu.VMEM)
    scalars = pl.BlockSpec(memory_space=pltpu.SMEM)
    anywhere = pl.BlockSpec(memory_space=pl.ANY)
    count = len(args)

    def body(*refs):
        kernel(*refs[:count], *refs[count + len(order) :])

    return pl.pallas_call(
        body,
        out_shape=outs,
        in_specs=[scalars] * smem + [vmem] * (count - smem) + [anywhere] * len(order),
        out_specs=[anywhere if left_out else vmem] * len(outs),
        scratch_shapes=list(scratch),
        compiler_params=pltpu.CompilerParams(vmem_limit_bytes=mib * MIB),
        name=name,
    )(*args, *order)


def roles(band, strided):
    role = lax.axis_index("dp")
    pl.when(role == 0)(band)
    pl.when(role == 1)(strided)


def spot(g):
    place = lax.axis_index("seq")
    return lax.div(place, g), lax.rem(place, g)


def read_field(own_ref, other_ref, att_ref, i, t):
    if t == 3:
        return lambda rows, lanes: att_ref[i, rows, lanes]
    return lambda rows, lanes: (own_ref, other_ref)[i][t, rows, lanes]


def pack_fields_kernel(g, own_ref, other_ref, att_ref, *out_refs):
    line, spot_ = spot(g)
    rows = own_ref.shape[1]
    chunk = rows // g
    fields = [(i, t, read_field(own_ref, other_ref, att_ref, i, t)) for i in range(2) for t in range(4)]

    def band():
        for d in range(1, g):
            for i, t, read in fields:
                at = (i * 4 + t) * rows
                out_refs[d - 1][at : at + rows] = read(slice(None), rows_at((spot_ ^ d) * HD, HD))

    def strided():
        for d in range(1, g):
            there = rows_at((line ^ d) * chunk, chunk)
            for i, t, read in fields:
                for h in range(HS):
                    at = (i * 4 + t) * rows + h * chunk
                    out_refs[d - 1][at : at + chunk] = read(there, slice(h * HD, (h + 1) * HD))

    roles(band, strided)


def att_grad_kernel(own_ref, other_ref, weight_ref, out_ref):
    out_ref[0] = nt(own_ref[...], weight_ref[...]).astype(BF)
    out_ref[1] = nt(other_ref[...], weight_ref[...]).astype(BF)


def strided_bias(rows, chunk, reach):
    key = lax.broadcasted_iota(jnp.int32, (rows, rows), 0)
    query = lax.broadcasted_iota(jnp.int32, (rows, rows), 1)
    apart = lax.div(query, chunk) - lax.div(key, chunk)
    same = lax.rem(key, chunk) == lax.rem(query, chunk)
    return jnp.where(same & (apart >= 0) & (apart < reach), 0.0, -1e30)


def score_grads(probs, probs_low, dprobs):
    delta = jnp.sum(probs_low.astype(F32) * dprobs, axis=0, keepdims=True)
    return (probs * (dprobs - delta)).astype(BF), delta


SCALE = HD ** (-0.5)
SCALE_2 = SCALE / math.log(2)


def softmax(scores, bias):
    scores = scores * SCALE_2 + bias
    peak = jnp.max(scores, axis=0, keepdims=True)
    raised = jnp.exp2(scores - peak)
    total = jnp.sum(raised, axis=0, keepdims=True)
    return raised * (1.0 / total), peak + jnp.log2(total)


def forward_kernel(g, reach_ref, own_ref, other_ref, att_ref, r1_ref, r2_ref, r3_ref,
                   fqg_ref, fkv_ref, o1_ref, o2_ref, o3_ref, keep_ref, grads_ref):
    line, spot_ = spot(g)
    rows = own_ref.shape[1]
    span = g * rows
    chunk = rows // g
    came = (r1_ref, r2_ref, r3_ref)
    back = (o1_ref, o2_ref, o3_ref)
    fields = [(i, t, read_field(own_ref, other_ref, att_ref, i, t)) for i in range(2) for t in range(4)]

    def put(i, t, start, size, value):
        ref = (fqg_ref, fkv_ref, fkv_ref, fqg_ref)[t]
        ref[rows_at((t // 2 * 2 + i) * span + start, size)] = value

    def band():
        for i, t, read in fields:
            at = (i * 4 + t) * rows
            put(i, t, spot_ * rows, rows, read(slice(None), rows_at(spot_ * HD, HD)))
            for d in range(1, g):
                put(i, t, (spot_ ^ d) * rows, rows, came[d - 1][at : at + rows])

    def strided():
        here = rows_at(line * chunk, chunk)
        for i, t, read in fields:
            for h in range(HS):
                at = (i * 4 + t) * rows + h * chunk
                put(i, t, h * rows + line * chunk, chunk, read(here, slice(h * HD, (h + 1) * HD)))
                for d in range(1, g):
                    put(i, t, h * rows + (line ^ d) * chunk, chunk, came[d - 1][at : at + chunk])
        each = [(i, h) for h in range(HS) for i in range(2)]

        def head(t, i, h):
            at = (t // 2 * 2 + i) * span + h * rows
            return (fqg_ref, fkv_ref, fkv_ref, fqg_ref)[t][at : at + rows]

        scores, dprobs, probs = {}, {}, {}
        for i, h in each:
            scores[i, h] = nt(head(1, i, h), head(0, i, h))
            dprobs[i, h] = nt(head(2, i, h), head(3, i, h))
        for h in range(HS):
            bias = strided_bias(rows, chunk, reach_ref[h])
            for i in range(2):
                probs[i, h], _ = softmax(scores[i, h], bias)
        for i, h in each:
            keep_ref[i, h] = tn(probs[i, h].astype(BF), head(2, i, h)).astype(BF)
        for d in range(1, g):
            there = rows_at((line ^ d) * chunk, chunk)
            for i, h in each:
                at = (i * HS + h) * chunk
                back[d - 1][at : at + chunk] = keep_ref[i, h, there]
        for i, h in each:
            mine = slice(h * rows, (h + 1) * rows)
            probs_low = probs[i, h].astype(BF)
            dscores, _ = score_grads(probs[i, h], probs_low, dprobs[i, h])
            grads_ref[i, 0, mine] = (tn(dscores, head(1, i, h)) * SCALE).astype(BF)
            grads_ref[i, 1, mine] = (nn(dscores, head(0, i, h)) * SCALE).astype(BF)
            grads_ref[i, 2, mine] = nn(probs_low, head(3, i, h)).astype(BF)

    roles(band, strided)


def heads_kernel(g, keep_ref, o1_ref, o2_ref, o3_ref, p1_ref, p2_ref, p3_ref, mine_ref):
    line, spot_ = spot(g)
    rows = keep_ref.shape[2]
    chunk = rows // g
    came = (o1_ref, o2_ref, o3_ref)
    outs = (mine_ref, p1_ref, p2_ref, p3_ref)

    def strided():
        for to in range(g):
            head = spot_ ^ to
            for i in range(2):
                outs[to][rows_at(i * rows + line * chunk, chunk)] = keep_ref[i, head, rows_at(line * chunk, chunk)]
                for d in range(1, g):
                    source = rows_at((i * HS + head) * chunk, chunk)
                    outs[to][rows_at(i * rows + (line ^ d) * chunk, chunk)] = came[d - 1][source]

    roles(lambda: None, strided)


def attention_kernel(g, width_ref, fqg_ref, fkv_ref, halo_ref,
                     out_ref, dquery_ref, dkv_ref, stats_ref, key_s, value_s, key_t, value_t):
    line, spot_ = spot(g)
    span = dquery_ref.shape[1]
    rows = span // g

    def band():
        width = width_ref[spot_]
        key_at = lax.broadcasted_iota(jnp.int32, (span + rows, rows), 0)
        query_at = lax.broadcasted_iota(jnp.int32, (span + rows, rows), 1)
        block = lax.div(key_at, BLK)
        near = (block >= WMAX - width) & (key_at - span <= query_at)
        for i in range(2):
            for t, ref in enumerate((key_s, value_s)):
                at = (t * 2 + i) * span
                ref[i, span:] = fkv_ref[at : at + span]
                ref[i, :span] = halo_ref[at : at + span]
            key_t[i] = key_s[i].T
            value_t[i] = value_s[i].T
        for last in range(g - 1, 0, -2):
            chains = [(b, i) for b in (last, last - 1) for i in range(2)]
            each = range(len(chains))
            bias = [jnp.where(near & ((block + b >= g) | (line > 0)), 0.0, -1e30) for b in (last, last - 1)]
            window = [slice(b * rows, b * rows + span + rows) for b, _ in chains]
            mine = [slice(b * rows, (b + 1) * rows) for b, _ in chains]
            own = [slice(span - b * rows, span + rows) for b, _ in chains]
            query = [fqg_ref[i * span + b * rows : i * span + (b + 1) * rows] for b, i in chains]
            grad = [fqg_ref[(2 + i) * span + b * rows : (2 + i) * span + (b + 1) * rows] for b, i in chains]
            scores = [nt(key_s[chains[n][1], window[n]], query[n]) for n in each]
            dprobs = [nt(value_s[chains[n][1], window[n]], grad[n]) for n in each]
            probs, total = zip(*[softmax(scores[n], bias[n // 2]) for n in each])
            probs_low = [probs[n].astype(BF) for n in each]
            outputs = [nn(value_t[chains[n][1], :, window[n]], probs_low[n]) for n in each]
            dvalue = [nn(probs_low[n][own[n]], grad[n]) for n in each]
            dscores, delta = zip(*[score_grads(probs[n], probs_low[n], dprobs[n]) for n in each])
            dquery = [nn(key_t[chains[n][1], :, window[n]], dscores[n]) for n in each]
            dkey = [nn(dscores[n][own[n]], query[n]) * SCALE for n in each]
            for n, (b, i) in enumerate(chains):
                out_ref[i, :, mine[n]] = outputs[n].astype(BF)
                stats_ref[i * 8 : i * 8 + 1, mine[n]] = total[n]
                stats_ref[i * 8 + 1 : i * 8 + 2, mine[n]] = delta[n]
                dquery_ref[i, mine[n]] = (dquery[n] * SCALE).astype(BF).T
                if b == g - 1:
                    dkv_ref[i, 0] = dkey[n]
                    dkv_ref[i, 1] = dvalue[n]
                else:
                    dkv_ref[i, 0, : (b + 1) * rows] += dkey[n]
                    dkv_ref[i, 1, : (b + 1) * rows] += dvalue[n]

    roles(band, lambda: None)


def tail_kernel(g, width_ref, fkv_ref, next_ref, stats_ref, dkv_ref, out_ref):
    line, spot_ = spot(g)
    span = dkv_ref.shape[2]
    rows = span // g

    def band():
        out_ref[...] = dkv_ref[...]

        @pl.when(line < g - 1)
        def _():
            width = width_ref[spot_]
            for first in range(0, g, 2):
                chains = [(b, i) for b in (first, first + 1) for i in range(2)]
                each = range(len(chains))
                bias = []
                for b in (first, first + 1):
                    block = lax.div(lax.broadcasted_iota(jnp.int32, (span - b * rows, rows), 0), BLK)
                    bias.append(jnp.where(block >= WMAX - width, 0.0, -1e30))
                mine = [slice(b * rows, (b + 1) * rows) for b, _ in chains]
                query = [next_ref[i * span + b * rows : i * span + (b + 1) * rows] for b, i in chains]
                grad = [next_ref[(2 + i) * span + b * rows : (2 + i) * span + (b + 1) * rows] for b, i in chains]
                scores = [nt(fkv_ref[i * span + b * rows : (i + 1) * span], query[n]) for n, (b, i) in enumerate(chains)]
                dprobs = [
                    nt(fkv_ref[(2 + i) * span + b * rows : (3 + i) * span], grad[n]) for n, (b, i) in enumerate(chains)
                ]
                probs = [
                    jnp.exp2(scores[n] * SCALE_2 + bias[n // 2] - stats_ref[i * 8 : i * 8 + 1, mine[n]])
                    for n, (_, i) in enumerate(chains)
                ]
                dvalue = [nn(probs[n].astype(BF), grad[n]) for n in each]
                dscores = [
                    (probs[n] * (dprobs[n] - stats_ref[i * 8 + 1 : i * 8 + 2, mine[n]])).astype(BF)
                    for n, (_, i) in enumerate(chains)
                ]
                dkey = [nn(dscores[n], query[n]) * SCALE for n in each]
                for n, (b, i) in enumerate(chains):
                    out_ref[i, 0, b * rows :] += dkey[n]
                    out_ref[i, 1, b * rows :] += dvalue[n]

    roles(band, lambda: None)


def copy_kernel(in_ref, out_ref):
    out_ref[...] = in_ref[...]


def weight_kernel(g, out_ref, *refs):
    heads, (og_ref, og_other_ref), near = refs[:g], refs[g : g + 2], refs[g + 2 : -g - 1]
    part_ref, z_refs, sum_s = refs[-g - 1], refs[-g:-1], refs[-1]
    line, spot_ = spot(g)
    rows = og_ref.shape[0]
    chunk = rows // g
    outer = ((og_ref, *near[: g - 1]), (og_other_ref, *near[g - 1 :]))

    def add(part):
        sum_s[...] = sum(part(i, d) for i in range(2) for d in range(g))

    roles(
        lambda: add(lambda i, d: nn(out_ref[i, :, rows_at((spot_ ^ d) * rows, rows)], outer[i][d][...])),
        lambda: add(lambda i, d: tn(heads[d][i * rows : (i + 1) * rows], outer[i][d][...])),
    )
    part_ref[...] = sum_s[rows_at(line * chunk, chunk)]
    for d, ref in enumerate(z_refs, 1):
        ref[...] = sum_s[rows_at((line ^ d) * chunk, chunk)].astype(BF)


def exchange_kernel(dquery_ref, dkv_ref, strided_ref, keep_ref, *rest):
    piece_refs, send_s = rest[:-1], rest[-1]

    def band():
        for i, ref in enumerate((keep_ref, send_s)):
            ref[0] = dquery_ref[i]
            ref[1] = dkv_ref[i, 0].astype(BF)
            ref[2] = dkv_ref[i, 1].astype(BF)

    def strided():
        keep_ref[...] = strided_ref[0]
        send_s[...] = strided_ref[1]

    roles(band, strided)
    size = piece_refs[0].shape[1]
    for n, ref in enumerate(piece_refs):
        ref[...] = send_s[:, n * size : (n + 1) * size]


def sum_kernel(keep_ref, z1_ref, z2_ref, z3_ref, out_ref):
    total = keep_ref[...]
    for ref in (z1_ref, z2_ref, z3_ref):
        total += ref[...].astype(F32)
    out_ref[...] = total.astype(BF)


def gather_kernel(g, pieces, own_ref, g1_ref, g2_ref, g3_ref, keep_ref, *refs):
    line, spot_ = spot(g)
    swapped_refs, out_refs, swapped = refs[:pieces], refs[pieces:-1], refs[-1]
    half_span = swapped_refs[0].shape[1]
    for n, ref in enumerate(swapped_refs):
        swapped[:, n * half_span : (n + 1) * half_span] = ref[...]
    size, width = own_ref.shape
    span = keep_ref.shape[1]
    rows = span // g
    chunk = rows // g
    columns = width // HD
    to_group, to_line = out_refs[:g], out_refs[g:]
    for d, ref in enumerate((own_ref, g1_ref, g2_ref, g3_ref)):
        for n in range(columns):
            for out_ref in to_group:
                out_ref[rows_at(n * g * size + (line ^ d) * size, size)] = ref[:, n * HD : (n + 1) * HD]

    def grads(band, strided):
        for d in range(g):
            for t in range(3):
                at = columns * g * size + t * rows
                to_group[d][at : at + rows] = band[t, rows_at((spot_ ^ d) * rows, rows)]
                for h in range(HS):
                    there = rows_at(h * rows + (line ^ d) * chunk, chunk)
                    to_line[d][(t * HS + h) * chunk : (t * HS + h + 1) * chunk] = strided[t, there]

    roles(lambda: grads(keep_ref, swapped), lambda: grads(swapped, keep_ref))


def finish_kernel(g, *refs):
    from_group, from_line = refs[:g], refs[g : 2 * g]
    outs, weight_ref, grads_s, weight_s, sems = refs[2 * g : 2 * g + 3], *refs[2 * g + 3 :]
    line, spot_ = spot(g)
    rows, width = grads_s.shape[1:]
    half = width // 2
    chunk = rows // g
    size = weight_s.shape[0] // g
    columns = width // HD
    copies = []
    for t in range(3):
        for d in range(g):
            at = columns * size + t * rows
            grads_s[t, :, rows_at((spot_ ^ d) * HD, HD)] = from_group[d][at : at + rows]
            for h in range(HS):
                lanes = slice(half + h * HD, half + (h + 1) * HD)
                at = (t * HS + h) * chunk
                grads_s[t, rows_at((line ^ d) * chunk, chunk), lanes] = from_line[d][at : at + chunk]
        copies.append(pltpu.make_async_copy(grads_s.at[t], outs[t], sems.at[t]))
        copies[-1].start()
    for d in range(g):
        there = rows_at((spot_ ^ d) * size, size)
        for n in range(columns):
            weight_s[there, n * HD : (n + 1) * HD] = from_group[d][n * size : (n + 1) * size]
        copies.append(pltpu.make_async_copy(weight_s.at[there], weight_ref.at[there], sems.at[3 + d]))
        copies[-1].start()
    for copy in copies:
        copy.wait()


def body_roles(g, queries, keys, values, out_grad, out_weight, band_width, col_reach):
    q, k, v, og = queries[0], keys[0], values[0], out_grad[0]
    rows, width = q.shape
    half = width // 2
    span = g * rows
    chunk = rows // g
    devices = lax.axis_size("seq")
    both = ("dp", "seq")

    def send(value, target):
        pairs = []
        for role in range(2):
            for line in range(g):
                for place in range(g):
                    to = target(role, line, place)
                    if to is None:
                        continue
                    to_role, to_line, to_place = to
                    pairs.append((role * devices + line * g + place, to_role * devices + to_line * g + to_place))
        return lax.ppermute(value, both, pairs)

    def swap(value):
        return lax.ppermute(value, "dp", [(0, 1), (1, 0)])

    def by_role(d):
        return lambda role, line, place: (0, line, place ^ d) if role == 0 else (1, line ^ d, place)

    def along_line(d):
        return lambda role, line, place: (role, line ^ d, place)

    def in_group(d):
        return lambda role, line, place: (role, line, place ^ d)

    def shift(step):
        return lambda role, line, place: (0, line + step, place) if role == 0 and 0 <= line + step < g else None

    def ring(step):
        def target(role, line, place):
            to = line + (step if role == 0 else -step)
            return (role, to, place) if 0 <= to < g else (1 - role, line, place)

        return target

    steps = range(1, g)
    role = lax.axis_index("dp")
    og_other = swap(og)
    to_other = jnp.stack([lax.dynamic_slice(value, (0, (1 - role) * half), (rows, half)) for value in (q, k, v)])
    own = jnp.stack([lax.dynamic_slice(value, (0, role * half), (rows, half)) for value in (q, k, v)])
    other = swap(to_other)
    (att,) = call(att_grad_kernel, [shaped((2, rows, half))], [og, og_other, out_weight], name="att_grad")
    packed = call(functools.partial(pack_fields_kernel, g), [shaped((8 * rows, HD))] * (g - 1),
                  [own, other, att], name="pack_fields")
    came = [send(packed[d - 1], by_role(d)) for d in steps]
    near = [send(og, in_group(d)) for d in steps]
    near_other = [swap(value) for value in near]
    fqg, fkv, *back, keep, strided_grads = call(
        functools.partial(forward_kernel, g),
        [shaped((4 * span, HD))] * 2 + [shaped((2 * rows, HD))] * (g - 1)
        + [shaped((2, HS, rows, HD)), shaped((2, 3, span, HD))],
        [col_reach, own, other, att] + came, smem=1, name="forward",
    )
    back = [send(back[d - 1], by_role(d)) for d in steps]
    halo = send(fkv, shift(1))
    *to_heads, mine = call(functools.partial(heads_kernel, g), [shaped((2 * rows, HD))] * g, [keep] + back,
                           name="heads")
    band_out, dquery, dkv, stats = call(
        functools.partial(attention_kernel, g),
        [shaped((2, HD, span)), shaped((2, span, HD)), shaped((2, 2, span, HD), F32), shaped((48, span), F32)],
        [band_width, fqg, fkv, halo], smem=1,
        scratch=[pltpu.VMEM((2, 2 * span, HD), BF), pltpu.VMEM((2, 2 * span, HD), BF),
                 pltpu.VMEM((2, HD, 2 * span), BF), pltpu.VMEM((2, HD, 2 * span), BF)],
        mib=24, name="attention",
    )
    (fqg_copy,) = call(copy_kernel, [shaped(fqg.shape)], [fqg], name="copy")
    following = send(fqg_copy, shift(-1))
    heads = [send(to_heads[d - 1], in_group(d)) for d in steps]
    piece = half // g // g
    parts = call(
        functools.partial(weight_kernel, g), [shaped((piece, width), F32)] + [shaped((piece, width))] * (g - 1),
        [band_out, mine] + heads + [og, og_other] + near + near_other,
        scratch=[pltpu.VMEM((half // g, width), F32)], name="weight",
    )
    summed = [send(parts[d], along_line(d)) for d in steps]
    stats = send(stats, ring(-1))
    (dkv,) = call(functools.partial(tail_kernel, g), [shaped(dkv.shape, F32)],
                  [band_width, fkv, following, stats, dkv], smem=1, order=[summed[-1]], name="tail")
    (piece_sum,) = call(sum_kernel, [shaped((piece, width))], [parts[0]] + summed, order=[dkv], name="sum")
    pieces = [send(piece_sum, along_line(d)) for d in steps]
    grads_kept, *to_other = call(
        exchange_kernel, [shaped((3, span, HD))] + [shaped((3, span // 2, HD))] * 2,
        [dquery, dkv, strided_grads], order=[piece_sum], scratch=[pltpu.VMEM((3, span, HD), BF)], name="exchange",
    )
    packed = call(
        functools.partial(gather_kernel, g, len(to_other)),
        [shaped((half // g * width // HD + 3 * rows, HD))] * g + [shaped((3 * rows, HD))] * g,
        [piece_sum] + pieces + [grads_kept] + [swap(value) for value in to_other],
        scratch=[pltpu.VMEM((3, span, HD), BF)], name="gather_line",
    )
    from_group = [packed[0]] + [send(packed[d], in_group(d)) for d in steps]
    from_line = [packed[g]] + [send(packed[g + d], along_line(d)) for d in steps]
    dq, dk, dv, weight_grad = call(
        functools.partial(finish_kernel, g), [shaped((rows, width))] * 3 + [shaped((half, width))],
        from_group + from_line, left_out=True,
        scratch=[pltpu.VMEM((3, rows, width), BF), pltpu.VMEM((half, width), BF), pltpu.SemaphoreType.DMA((3 + g,))],
        name="finish",
    )
    return dq[None], dk[None], dv[None], weight_grad


def from_behind(value, axis, steps):
    count = lax.axis_size(axis)
    leading, last = (max(0, -steps), min(count, count - steps))
    return lax.ppermute(value, axis, [(source, source + steps) for source in range(leading, last)])


def attend(query_g, key_g, value_g, grad_g, allowed):
    scale = query_g.shape[-1] ** (-0.5)
    scores = jnp.einsum("gqd,gkd->gqk", query_g, key_g, preferred_element_type=F32) * scale
    scores = jnp.where(allowed, scores, -1e30)
    peak = jnp.max(scores, axis=-1, keepdims=True)
    raised = jnp.where(allowed, jnp.exp(scores - peak), 0.0)
    probs = raised / jnp.sum(raised, axis=-1, keepdims=True)
    probs_low = probs.astype(BF)
    output = jnp.einsum("gqk,gkd->gqd", probs_low, value_g, preferred_element_type=F32).astype(BF)
    delta = jnp.sum(grad_g.astype(F32) * output.astype(F32), axis=-1, keepdims=True)
    dprobs = jnp.einsum("gqd,gkd->gqk", grad_g, value_g, preferred_element_type=F32)
    dscores = (probs * (dprobs - delta)).astype(BF)
    d_query = jnp.einsum("gqk,gkd->gqd", dscores, key_g, preferred_element_type=F32) * scale
    d_key = jnp.einsum("gqk,gqd->gkd", dscores, query_g, preferred_element_type=F32) * scale
    d_value = jnp.einsum("gqk,gqd->gkd", probs_low, grad_g, preferred_element_type=F32)
    return (output, d_query, d_key, d_value)


def band_mask(q_pos, k_pos, width):
    lower = (q_pos // BLK)[None, :, None] - width[:, None, None]
    causal = k_pos[None, None, :] <= q_pos[None, :, None]
    inside = k_pos[None, None, :] >= 0
    return causal & inside & ((k_pos // BLK)[None, None, :] >= lower)


def column_mask(count, reach):
    row_q = jnp.arange(count, dtype=jnp.int32)[None, :, None]
    row_k = jnp.arange(count, dtype=jnp.int32)[None, None, :]
    return (row_k <= row_q) & (row_q - row_k < reach[:, None, None])


def column_local(field, reach, devices):
    per_dev = IMW // devices
    count = field.shape[1] // per_dev
    grid = (
        field.reshape(4, count, per_dev, HS, HD)
        .transpose(0, 2, 3, 1, 4)
        .reshape(4, per_dev * HS, count, HD)
    )
    allowed = jnp.tile(column_mask(count, reach), (per_dev, 1, 1))
    output, d_query, d_key, d_value = attend(grid[0], grid[1], grid[2], grid[3], allowed)
    stacked = jnp.stack([output, d_query.astype(BF), d_key.astype(BF), d_value.astype(BF)])
    stacked = stacked.reshape(4, per_dev, HS, count, HD).transpose(0, 3, 1, 2, 4)
    return stacked.reshape(4, count * per_dev, 1, HS, HD)


def heads_first(field, count):
    return field.reshape(count, HB, HD).transpose(1, 0, 2)


def rows_first(field, count):
    return field.transpose(1, 0, 2).reshape(count, HB * HD)


def body_any(queries, keys, values, out_grad, out_weight, band_width, col_reach):
    query_all = queries[0]
    key_all = keys[0]
    value_all = values[0]
    grad_out = out_grad[0]
    rows = query_all.shape[0]
    devices = lax.axis_size("seq")
    place = lax.axis_index("seq")
    band_dim = HB * HD
    att_grad = jnp.einsum(
        "to,ao->ta",
        grad_out,
        lax.all_gather(out_weight, "dp", axis=0, tiled=True),
        preferred_element_type=F32,
    ).astype(BF)
    strided = jnp.stack([field[:, band_dim:] for field in (query_all, key_all, value_all, att_grad)])
    strided = strided.reshape(4, rows // devices, devices, HS, HD)
    column_major = lax.all_to_all(strided, "seq", split_axis=2, concat_axis=1, tiled=True)
    column_result = column_local(column_major, col_reach, devices)
    row_major = lax.all_to_all(
        column_result, "seq", split_axis=1, concat_axis=2, tiled=True
    ).reshape(4, rows, HS * HD)
    kv_own = (key_all[:, :band_dim], value_all[:, :band_dim])
    reach_dev = -(-(WMAX * BLK) // rows)
    earlier = []
    for hop in range(reach_dev, 0, -1):
        earlier.append(from_behind((kv_own[0], kv_own[1]), "seq", hop))
    key_window = jnp.concatenate([pair[0] for pair in earlier] + [kv_own[0]], 0)
    value_window = jnp.concatenate([pair[1] for pair in earlier] + [kv_own[1]], 0)
    width_all = (reach_dev + 1) * rows
    q_pos = place * rows + jnp.arange(rows, dtype=jnp.int32)
    k_pos = (place - reach_dev) * rows + jnp.arange(width_all, dtype=jnp.int32)
    allowed = band_mask(q_pos, k_pos, band_width)
    band_out, band_dq, band_dk, band_dv = attend(
        heads_first(query_all[:, :band_dim], rows),
        heads_first(key_window, width_all),
        heads_first(value_window, width_all),
        heads_first(att_grad[:, :band_dim], rows),
        allowed,
    )
    key_rows = rows_first(band_dk, width_all)
    value_rows = rows_first(band_dv, width_all)
    key_total = key_rows[reach_dev * rows :]
    value_total = value_rows[reach_dev * rows :]
    for hop in range(1, reach_dev + 1):
        slot = (reach_dev - hop) * rows
        key_total += from_behind(key_rows[slot : slot + rows].astype(BF), "seq", -hop).astype(F32)
        value_total += from_behind(value_rows[slot : slot + rows].astype(BF), "seq", -hop).astype(F32)
    attn_out = jnp.concatenate([rows_first(band_out, rows), row_major[0]], 1)
    query_grad = jnp.concatenate([rows_first(band_dq, rows).astype(BF), row_major[1]], 1)
    key_grad = jnp.concatenate([key_total.astype(BF), row_major[2]], 1)
    value_grad = jnp.concatenate([value_total.astype(BF), row_major[3]], 1)
    shared = lax.psum_scatter(
        jnp.einsum("ta,to->ao", attn_out, grad_out, preferred_element_type=F32).astype(BF),
        "dp",
        scatter_dimension=0,
        tiled=True,
    ).astype(F32)
    weight_grad = lax.psum(shared, "seq")
    return (query_grad[None], key_grad[None], value_grad[None], weight_grad.astype(BF))


def solution(mesh):
    def body(*args):
        rows = args[0].shape[1]
        devices = mesh.shape["seq"]
        g = IMW // rows
        fits = (
            mesh.shape["dp"] == 2
            and rows == BLK
            and devices == g * g
            and g == HB == HS == 4
            and WMAX * BLK == IMW
            and args[4].shape[0] == HB * HD == HS * HD
        )
        return body_roles(g, *args) if fits else body_any(*args)

    return jax.shard_map(
        body,
        mesh=mesh,
        in_specs=(
            P("dp", "seq", None),
            P("dp", "seq", None),
            P("dp", "seq", None),
            P("dp", "seq", None),
            P("dp", None),
            P(),
            P(),
        ),
        out_specs=(P("dp", "seq", None), P("dp", "seq", None), P("dp", "seq", None), P("dp", None)),
        check_vma=False,
    )
```
